512 devices in a mesh: gx: 16 (over x, y_hi, core), gy: 16 (over z), gz: 2 (over y_lo).
Axes of the slice: x: 4, y: 4 (y_hi: 2, y_lo: 2; y = y_hi * 2 + y_lo), z: 16, core: 2. Of those that a mesh axis runs over, the one named last changes fastest.
Arguments:
- temps: float32 [3, 512, 256, 256], P(None, 'gx', 'gy', 'gz'), may hold values from 0.2 to 1.5
- cotangent: float32 [512, 256, 256], P('gx', 'gy', 'gz'), may hold values from -6 to 6
- solid_mask: int32 [512, 256, 256], P('gx', 'gy', 'gz'), may hold values from 0 to 1, as said below
- patch_ids: int32 [512, 256, 256], P('gx', 'gy', 'gz'), may hold values from 0 to 8191, as said below
- heat_coeff: float32 [8192], replicated, may hold values from 0.2 to 2
- owner_slot: int32 [8192], replicated, may hold values from 0 to 8191, each once
Outputs:
- sensitivity: float32 [512, 256, 256], P('gx', 'gy', 'gz')
- patch_grad: float32 [8192], P(('gx', 'gy', 'gz'))
The draws below stay inside these ranges and needn't reach their ends.
Inputs may be any that keep to these rules, and one draw needn't show every extreme that they name: `solid_mask`: in each column of 8 x 8 voxels at x and y multiples of 8, the milled voxels are those of depth index below a depth of that column (possibly 0 or all 256). patch_ids // 16 is (a * 16 + b) * 2 + c with a = ((x + 16) mod 512) // 32, b and c likewise along y and depth. `owner_slot`: each slot once.
All inputs are finite; a program needn't handle non-finite values.
Results may differ from the reference program's by a relative error of at most 0.0003.
Values sent between devices are 32-bit elements; how exact they have to be, the bound alone decides.
A program may use at most 64 MiB of HBM per device.

```python
import math
import jax
import jax.numpy as jnp
from jax import lax

CX = 32
CY = 16
CZ = 128
STEPS = 3
PATCH_PER = 16
NX = 512
NY = 256
NZ = 256
PATCHES = 8192


def draw_solid_mask(key, part):
    key = jax.random.fold_in(key, 11)
    first_key, second_key = jax.random.split(key)
    columns = (NX // 8, NY // 8)
    pocket_depth = jax.random.randint(first_key, columns, 0, NZ + 1)
    milled = jax.random.randint(second_key, columns, 0, 2)
    pocket_depth = pocket_depth * milled
    expanded = jnp.repeat(jnp.repeat(pocket_depth, 8, 0), 8, 1)
    heights = jnp.arange(NZ, dtype=jnp.int32)
    return (heights[None, None, :] >= expanded[:, :, None]).astype(jnp.int32)


def draw_patch_ids(key, part):
    key = jax.random.fold_in(key, 12)
    cell_x = (jnp.arange(NX, dtype=jnp.int32) + CX // 2) % NX // CX
    cell_y = (jnp.arange(NY, dtype=jnp.int32) + CY // 2) % NY // CY
    cell_z = (jnp.arange(NZ, dtype=jnp.int32) + CZ // 2) % NZ // CZ
    cells = (cell_x[:, None, None] * (NY // CY) + cell_y[None, :, None]) * (NZ // CZ) + cell_z[None, None, :]
    offsets = jax.random.randint(key, (NX, NY, NZ), 0, PATCH_PER)
    return (cells * PATCH_PER + offsets).astype(jnp.int32)


def block_levels(own_key, extent, shards, least, high):
    def one(position, shards_of):
        steps = jax.random.uniform(jax.random.fold_in(jax.random.fold_in(own_key, 6), position), (shards_of,), jnp.float32, least / len(shards), high / len(shards))
        return jnp.repeat(jnp.exp(steps), extent[position] // shards_of).reshape((-1,) + (1,) * (len(extent) - position - 1))

    gain = one(*shards[0])
    for cut in shards[1:]:
        gain = gain * one(*cut)
    return gain


def bell_draw(own_key, extent, deviation, limit, pieces=(), held_as=jnp.bfloat16):
    array = jax.random.normal(own_key, extent, jnp.float32) * deviation
    if len(pieces) > 0:
        array = block_levels(own_key, extent, pieces, -0.22, 0.18) * array
    return jnp.clip(array, min=-limit, max=limit).astype(held_as)


def setup_inputs(seed: int = 0) -> dict:
    seeds = jax.random.split(jax.random.key(seed), 7)
    temps = jnp.clip(0.2 + 1.3 * jax.random.uniform(seeds[0], (STEPS, NX, NY, NZ), jnp.float32) ** block_levels(seeds[0], (STEPS, NX, NY, NZ), ((1, 16), (2, 16), (3, 2)), -0.2, 0.2), 0.2, 1.5)
    cotangent = bell_draw(seeds[1], (NX, NY, NZ), 1.0, 6.0, ((0, 16), (1, 16), (2, 2)), jnp.float32)
    solid_mask = draw_solid_mask(jax.random.fold_in(seeds[6], 71), 0)
    patch_ids = draw_patch_ids(jax.random.fold_in(seeds[6], 71), 0)
    heat_coeff = jnp.clip(jnp.exp(jax.random.uniform(seeds[4], (PATCHES,), jnp.float32, math.log(0.2), math.log(2.0))), 0.2, 2.0)
    owner_slot = jax.random.permutation(seeds[5], PATCHES).astype(jnp.int32)
    return {"temps": temps, "cotangent": cotangent, "solid_mask": solid_mask, "patch_ids": patch_ids, "heat_coeff": heat_coeff, "owner_slot": owner_slot}


time_step = 0.12
conduct = 1.0
steepness = 0.5
ambient = 0.6


def neighbours(padded):
    return [padded[2:, 1:-1, 1:-1], padded[:-2, 1:-1, 1:-1],
            padded[1:-1, 2:, 1:-1], padded[1:-1, :-2, 1:-1],
            padded[1:-1, 1:-1, 2:], padded[1:-1, 1:-1, :-2]]


def adjoint_core(lam_here, masked_pad, temp_pad, mask_pad, heat_here):
    temp_here = temp_pad[1:-1, 1:-1, 1:-1]
    mask_here = mask_pad[1:-1, 1:-1, 1:-1]
    inflow = jnp.zeros_like(lam_here)
    active = jnp.zeros_like(lam_here)
    for temp_there, mask_there, masked_there in zip(neighbours(temp_pad), neighbours(mask_pad), neighbours(masked_pad)):
        face_cond = conduct * (1.0 + steepness * 0.5 * (temp_here * temp_here + temp_there * temp_there))
        slope_term = conduct * steepness * temp_here * (temp_there - temp_here)
        inflow = inflow + mask_there * (slope_term - face_cond) * lam_here + (face_cond - slope_term) * masked_there
        active = active + mask_there
    open_faces = 6.0 - active
    updated = lam_here + time_step * mask_here * (inflow - heat_here * open_faces * lam_here)
    patch_term = -time_step * mask_here * open_faces * (temp_here - ambient) * lam_here
    return updated, patch_term


def reference(temps, cotangent, solid_mask, patch_ids, heat_coeff, owner_slot):
    mask_f = solid_mask.astype(jnp.float32)
    mask_pad = jnp.pad(mask_f, 1)
    adjoint = cotangent
    total = jnp.zeros(cotangent.shape, jnp.float32)
    for back_step in range(STEPS):
        level = STEPS - 1 - back_step
        masked_pad = jnp.pad(mask_f * adjoint, 1)
        temp_pad = jnp.pad(temps[level], 1)

        def block(number, masked_pad=masked_pad, temp_pad=temp_pad, current=adjoint):
            start = (number * CX).astype(jnp.int32)

            def take_rows(source, length):
                return lax.dynamic_slice_in_dim(source, start, length, 0)

            heat_here = heat_coeff[take_rows(patch_ids, CX)]
            return adjoint_core(take_rows(current, CX), take_rows(masked_pad, CX + 2),
                                take_rows(temp_pad, CX + 2), take_rows(mask_pad, CX + 2), heat_here)

        updated, patch_term = lax.map(block, jnp.arange(NX // CX, dtype=jnp.int32))
        adjoint = updated.reshape(cotangent.shape)
        total = total + patch_term.reshape(cotangent.shape)
    slots = owner_slot[patch_ids]
    patch_grad = jax.ops.segment_sum(total.reshape(-1), slots.reshape(-1), num_segments=PATCHES)
    return adjoint, patch_grad
```

```python
import jax
import jax.numpy as jnp
from jax import lax
from jax.experimental import pallas as pl
from jax.experimental.pallas import tpu as pltpu
from jax.sharding import PartitionSpec as P

STEPS = 3
PATCH_PER = 16
GX, GY, GZ = 16, 16, 2
CX, CY, CZ = 32, 16, 128
Y0 = 8
F32 = jnp.float32
MESH = pl.DeviceIdType.MESH

time_step = 0.12
ambient = 0.6


def x_loop(unroll, body, init):
    def block(i, carry):
        for k in range(unroll):
            carry = body(i * unroll + k, carry)
        return carry

    return lax.fori_loop(0, CX // unroll, block, init)


def sublane_sums(parts, sub):
    for width in (4, 2, 1):
        upper = (sub // width) % 2 == 1
        merged = []
        half = len(parts) // 2
        for low, high in zip(parts[:half], parts[half:]):
            low = low + pltpu.roll(low, 8 - width, 0)
            high = high + pltpu.roll(high, width, 0)
            merged.append(jnp.where(upper, high, low))
        parts = merged
    return parts[0]


def kernel(
    temps, cot, mask, ids, heat, owner,
    sens, patch,
    tpad, lpad, mpad, idv, heatv, ownv, hv, mm, kk, pe, tot, outv,
    zsend, zrecv, arow, plane, rrow, zbuf,
    lsem, ssem, rsem, gsem, zsem,
):
    gx, gy, gz = lax.axis_index("gx"), lax.axis_index("gy"), lax.axis_index("gz")
    here = gx * GZ + gz

    def in_plane(r):
        j = lax.rem(here + r, GX * GZ)
        return (j // GZ, gy, lax.rem(j, GZ))

    def in_column(r):
        return (gx, lax.rem(gy + r + GY, GY), gz)

    x_up, x_down = (lax.rem(gx + 1, GX), gy, gz), (lax.rem(gx + GX - 1, GX), gy, gz)
    y_up, y_down = in_column(1), in_column(-1)
    z_other = (gx, gy, 1 - gz)

    barrier = pltpu.get_barrier_semaphore()
    for r in range(1, GX * GZ):
        pl.semaphore_signal(barrier, inc=1, device_id=in_plane(r), device_id_type=MESH)
    near = (1, -1, 2, -2, 3, -3, 4, -4)
    for r in near:
        pl.semaphore_signal(barrier, inc=1, device_id=in_column(r), device_id_type=MESH)

    inner = (pl.ds(1, CX), pl.ds(Y0, CY))
    loads = [
        (ids, idv), (heat, heatv), (owner, ownv), (mask, mpad.at[inner]),
        (cot, lpad.at[0].at[inner]),
        (temps.at[2], tpad.at[2].at[inner]),
        (temps.at[1], tpad.at[1].at[inner]),
        (temps.at[0], tpad.at[0].at[inner]),
    ]
    loads = [pltpu.make_async_copy(s, d, lsem.at[i]) for i, (s, d) in enumerate(loads)]
    for c in loads:
        c.start()
    for c in loads:
        c.wait()

    lane = lax.broadcasted_iota(jnp.int32, (CY, CZ), 1)
    row = lax.broadcasted_iota(jnp.int32, (CY, CZ), 0)
    lane8 = lax.broadcasted_iota(jnp.int32, (8, CZ), 1)
    sub8 = lax.broadcasted_iota(jnp.int32, (8, CZ), 0)
    edge = jnp.where(gz == 0, CZ - 1, 0)

    def to_lane(value, target):
        return pltpu.roll(value, lax.rem(target - edge + CZ, CZ), 1)

    def from_lane(packed, source):
        return pltpu.roll(packed, lax.rem(edge - source + CZ, CZ), 1)

    zero = jnp.zeros((CY, CZ), F32)

    def before(x, carry):
        first, second = carry
        a = lax.rem(gx + x // (CX // 2), GX)
        picked = []
        for half in range(2):
            b = lax.rem(gy + half, GY)
            table = jnp.broadcast_to(heatv[pl.ds(a * 4 + b // 4, 1), :], (8, CZ))
            index = jnp.bitwise_and(idv[x, half * 8 : half * 8 + 8, :], CZ - 1)
            picked.append(jnp.take_along_axis(table, index, axis=1))
        hv[x] = jnp.concatenate(picked, axis=0)
        ins = pl.ds(Y0, CY)
        first = jnp.where(lane == x, to_lane(lpad[0, x + 1, ins, :], x), first)
        first = jnp.where(lane == x + 32, to_lane(tpad[2, x + 1, ins, :], x + 32), first)
        first = jnp.where(lane == x + 64, to_lane(mpad[x + 1, ins, :].astype(F32), x + 64), first)
        second = jnp.where(lane == x, to_lane(tpad[1, x + 1, ins, :], x), second)
        second = jnp.where(lane == x + 32, to_lane(tpad[0, x + 1, ins, :], x + 32), second)
        return first, second

    first, second = x_loop(4, before, (zero, zero))
    zsend[0] = first
    zsend[1] = second

    b0, b1 = gy, lax.rem(gy + 1, GY)
    s0 = ownv[pl.ds(b0 // 4, GX, stride=4), :]
    s1 = ownv[pl.ds(b1 // 4, GX, stride=4), :]
    s0 = pltpu.roll(s0, lax.rem(CZ - lax.rem(b0, 4) * 32, CZ), 1)
    s1 = pltpu.roll(s1, lax.rem(CZ + 32 - lax.rem(b1, 4) * 32, CZ), 1)
    s16 = jnp.where(lane < 32, s0, s1)
    slots = jnp.where(lane8 < 64, s16[:8], pltpu.roll(s16[8:], 64, 1))

    pl.semaphore_wait(barrier, GX * GZ - 1 + len(near))

    counter = [0]

    def remote(src, dst, device):
        i = counter[0]
        counter[0] += 1
        copy = pltpu.make_async_remote_copy(
            src_ref=src, dst_ref=dst, send_sem=ssem.at[i], recv_sem=rsem.at[i],
            device_id=device, device_id_type=MESH,
        )
        copy.start()
        return copy

    def x_faces(ref):
        ins = pl.ds(Y0, CY)
        return [
            remote(ref.at[CX, ins], ref.at[0, ins], x_up),
            remote(ref.at[1, ins], ref.at[CX + 1, ins], x_down),
        ]

    def y_faces(ref):
        ins = pl.ds(1, CX)
        return [
            remote(ref.at[ins, pl.ds(Y0 + CY - 1, 1)], ref.at[ins, pl.ds(Y0 - 1, 1)], y_up),
            remote(ref.at[ins, pl.ds(Y0, 1)], ref.at[ins, pl.ds(Y0 + CY, 1)], y_down),
        ]

    def z_face(i):
        return [remote(zsend.at[i], zrecv.at[i], z_other)]

    sent = []

    def landed(copies):
        sent.extend(copies)
        for c in copies:
            c.wait_recv()

    head = [mpad, lpad.at[0], tpad.at[2]]
    round_1 = sum([x_faces(r) for r in head], []) + z_face(0) + sum([y_faces(r) for r in head], [])
    tail = [tpad.at[1], tpad.at[0]]
    later_1 = [x_faces(tail[0]) + y_faces(tail[0]) + z_face(1), x_faces(tail[1]) + y_faces(tail[1])]
    for r in (4, -4):
        pl.semaphore_signal(zsem, inc=1, device_id=in_column(r), device_id_type=MESH)
    landed(round_1)

    def z_neighbours(value, halo):
        up = jnp.where(lane == CZ - 1, halo, pltpu.roll(value, CZ - 1, 1))
        down = jnp.where(lane == 0, halo, pltpu.roll(value, 1, 1))
        return up, down

    def six(ref, x, halo):
        ins = pl.ds(Y0, CY)
        here = ref[x + 1, ins, :]
        up, down = z_neighbours(here, halo)
        return here, [
            ref[x + 2, ins, :], ref[x, ins, :],
            ref[x + 1, pl.ds(Y0 + 1, CY), :], ref[x + 1, pl.ds(Y0 - 1, CY), :],
            up, down,
        ]

    inside = lambda cond: jnp.where(cond, 1.0, 0.0).astype(F32)
    keep_y_up = jnp.where(row == CY - 1, inside(gy < GY - 1), 1.0)
    keep_y_down = jnp.where(row == 0, inside(gy > 0), 1.0)
    keep_z_up = jnp.where(lane == CZ - 1, inside(gz == 0), 1.0)
    keep_z_down = jnp.where(lane == 0, inside(gz == 1), 1.0)

    def masks(x):
        halo = from_lane(zrecv[0], x + 64)
        ins = pl.ds(Y0, CY)
        centre = mpad[x + 1, ins, :].astype(F32)
        up, down = z_neighbours(centre, halo)
        others = [
            mpad[x + 2, ins, :].astype(F32) * inside((x < CX - 1) | (gx < GX - 1)),
            mpad[x, ins, :].astype(F32) * inside((x > 0) | (gx > 0)),
            mpad[x + 1, pl.ds(Y0 + 1, CY), :].astype(F32) * keep_y_up,
            mpad[x + 1, pl.ds(Y0 - 1, CY), :].astype(F32) * keep_y_down,
            up * keep_z_up,
            down * keep_z_down,
        ]
        active = others[0]
        for m in others[1:]:
            active = active + m
        scaled = time_step * centre
        surface = scaled * (6.0 - active)
        pe[x] = surface
        faces = [scaled * m for m in others]
        for d in range(6):
            mm[d, x] = faces[d]
        return faces, surface

    def coefficients(level, x, halo, faces, surface):
        here, there = six(tpad.at[level], x, halo)
        base = 1.0 + 0.75 * (here * here)
        half = 0.5 * here
        centre = 1.0 - surface * hv[x]
        out = []
        for t, m in zip(there, faces):
            k = m * (base + t * (0.25 * t - half))
            centre = centre - k
            out.append(k)
        return out, centre, here

    def apply(number, x, halo, out, centre):
        here, there = six(lpad.at[number], x, halo)
        new = centre * here
        for k, l in zip(out, there):
            new = new + k * l
        return new, here

    def step_1(x, packed):
        faces, surface = masks(x)
        out, centre, t = coefficients(2, x, from_lane(zrecv[0], x + 32), faces, surface)
        new, old = apply(0, x, from_lane(zrecv[0], x), out, centre)
        tot[x] = (t - ambient) * old
        lpad[1, x + 1, pl.ds(Y0, CY), :] = new
        return jnp.where(lane == x, to_lane(new, x), packed)

    zsend[2] = x_loop(4, step_1, zero)
    round_2 = x_faces(lpad.at[1]) + y_faces(lpad.at[1]) + z_face(2)

    def prepare(level, source):
        def body(x, carry):
            faces = [mm[d, x] for d in range(6)]
            out, centre, t = coefficients(level, x, from_lane(zrecv[1], x + source), faces, pe[x])
            for d in range(6):
                kk[d, x] = out[d]
            kk[6, x] = centre
            tot[x] = tot[x] + (t - ambient) * lpad[2 - level, x + 1, pl.ds(Y0, CY), :]
            return carry

        x_loop(4, body, 0)

    landed(later_1[0])
    prepare(1, 0)
    landed(round_2)

    def step_2(x, packed):
        new, _ = apply(1, x, from_lane(zrecv[2], x), [kk[d, x] for d in range(6)], kk[6, x])
        lpad[2, x + 1, pl.ds(Y0, CY), :] = new
        t0 = tpad[0, x + 1, pl.ds(Y0, CY), :]
        tot[x] = -pe[x] * (tot[x] + (t0 - ambient) * new)
        return jnp.where(lane == x, to_lane(new, x), packed)

    zsend[3] = x_loop(4, step_2, zero)

    by_depth = [jnp.where(lane8 // (CZ // 2) == (gz if c == 0 else 1 - gz), 1.0, 0.0) for c in range(2)]
    rows = []
    for xh in range(2):
        def gather(i, accs):
            for k in range(2):
                x = xh * (CX // 2) + 2 * i + k
                value = tot[x]
                offset = jnp.bitwise_and(idv[x], PATCH_PER - 1)
                accs = [acc + jnp.where(offset == o, value, 0.0) for o, acc in enumerate(accs)]
            return accs

        accs = lax.fori_loop(0, CX // 4, gather, [zero] * PATCH_PER)
        for yh in range(2):
            parts = [a[yh * 8 : yh * 8 + 8] for a in accs]
            low, high = sublane_sums(parts[:8], sub8), sublane_sums(parts[8:], sub8)
            for c in range(2):
                rows += [low * by_depth[c], high * by_depth[c]]
    rows = jnp.concatenate(rows, axis=0)
    across = (((1,), (1,)), ((), ()))
    message = lax.dot_general(
        jnp.ones((8, CZ), F32), rows, across,
        precision=lax.Precision.HIGHEST, preferred_element_type=F32,
    )
    arow[...] = message

    own_row = gz * GX + gx
    for r in range(1, GX * GZ):
        pltpu.make_async_remote_copy(
            src_ref=arow.at[pl.ds(0, 1)], dst_ref=plane.at[pl.ds(own_row, 1)],
            send_sem=gsem.at[0], recv_sem=gsem.at[1],
            device_id=in_plane(r), device_id_type=MESH,
        ).start()
    round_3 = x_faces(lpad.at[2]) + y_faces(lpad.at[2]) + z_face(3)
    landed(later_1[1])
    prepare_0 = lambda x: coefficients(
        0, x, from_lane(zrecv[1], x + 32), [mm[d, x] for d in range(6)], pe[x]
    )

    count = pl.ds(0, GX * GZ - 1)
    pltpu.make_async_copy(plane.at[count], plane.at[count], gsem.at[1]).wait()
    row32 = lax.broadcasted_iota(jnp.int32, (GX * GZ, CZ), 0)
    sums = jnp.where(row32 == own_row, message[:1], plane[...])
    sums = sums[:GX] + sums[GX:]
    shifted = pltpu.roll(sums, 64, 1)
    sums = sums + jnp.concatenate([shifted[GX - 1 :], shifted[: GX - 1]], axis=0)
    sums = jnp.where(lane8 < 64, sums[:8], pltpu.roll(sums[8:], 64, 1))

    mine = jnp.where((slots // 512 == gx) & (lax.rem(slots // 16, 2) == gz), sums, 0.0)
    target = lax.rem(slots // 32, GY)
    place = lax.rem(slots, PATCH_PER)
    values, marks = [], []
    for r in range(8):
        values.append(jnp.where(target[r : r + 1] == row, mine[r : r + 1], 0.0))
        marks.append(jnp.where(place[r : r + 1] == row, 1.0, 0.0))
    share = lax.dot_general(
        jnp.concatenate(values, axis=1),
        jnp.concatenate([jnp.concatenate([m, jnp.zeros((CZ - GY, CZ), F32)], axis=0) for m in marks], axis=1),
        across, precision=lax.Precision.HIGHEST, preferred_element_type=F32,
    )
    rrow[...] = share
    pl.semaphore_wait(zsem, 2)
    for r in range(1, GY):
        to = in_column(r)
        pltpu.make_async_remote_copy(
            src_ref=rrow.at[pl.ds(to[1], 1)], dst_ref=zbuf.at[pl.ds(gy, 1)],
            send_sem=gsem.at[2], recv_sem=gsem.at[3],
            device_id=to, device_id_type=MESH,
        ).start()

    landed(round_3)

    def step_3(x, carry):
        out, centre, _ = prepare_0(x)
        new, _ = apply(2, x, from_lane(zrecv[3], x), out, centre)
        outv[x] = new
        return carry

    x_loop(4, step_3, 0)
    store = pltpu.make_async_copy(outv, sens, lsem.at[0])
    store.start()
    for c in sent:
        c.wait_send()
    pltpu.make_async_copy(plane.at[count], plane.at[count], gsem.at[0]).wait()
    store.wait()
    count = pl.ds(0, GY - 1)
    pltpu.make_async_copy(zbuf.at[count], zbuf.at[count], gsem.at[3]).wait()
    final = jnp.where(row == gy, share, zbuf[...])
    patch[...] = jnp.sum(final, axis=0, keepdims=True)
    pltpu.make_async_copy(zbuf.at[count], zbuf.at[count], gsem.at[2]).wait()


def on_device(temps, cotangent, solid_mask, patch_ids, heat_coeff, owner_slot):
    anywhere = pl.BlockSpec(memory_space=pl.ANY)
    vmem = pl.BlockSpec(memory_space=pltpu.VMEM)
    field = (CX, CY, CZ)
    copies = 12 + 2 + 4 * 2 + 2 * 5
    sens, patch = pl.pallas_call(
        kernel,
        name="adjoint",
        out_shape=(
            jax.ShapeDtypeStruct(field, F32),
            jax.ShapeDtypeStruct((1, CZ), F32),
        ),
        in_specs=[anywhere] * 6,
        out_specs=(anywhere, vmem),
        scratch_shapes=[
            pltpu.VMEM((3, CX + 2, CY + 16, CZ), F32),
            pltpu.VMEM((3, CX + 2, CY + 16, CZ), F32),
            pltpu.VMEM((CX + 2, CY + 16, CZ), jnp.int32),
            pltpu.VMEM(field, jnp.int32),
            pltpu.VMEM((64, CZ), F32),
            pltpu.VMEM((64, CZ), jnp.int32),
            pltpu.VMEM(field, F32),
            pltpu.VMEM((6,) + field, F32),
            pltpu.VMEM((7,) + field, F32),
            pltpu.VMEM(field, F32),
            pltpu.VMEM(field, F32),
            pltpu.VMEM(field, F32),
            pltpu.VMEM((4, CY, CZ), F32),
            pltpu.VMEM((4, CY, CZ), F32),
            pltpu.VMEM((8, CZ), F32),
            pltpu.VMEM((GX * GZ, CZ), F32),
            pltpu.VMEM((GY, CZ), F32),
            pltpu.VMEM((GY, CZ), F32),
            pltpu.SemaphoreType.DMA((8,)),
            pltpu.SemaphoreType.DMA((copies,)),
            pltpu.SemaphoreType.DMA((copies,)),
            pltpu.SemaphoreType.DMA((4,)),
            pltpu.SemaphoreType.REGULAR,
        ],
        compiler_params=pltpu.CompilerParams(
            collective_id=0, has_side_effects=True, vmem_limit_bytes=40 * 1024 * 1024
        ),
    )(
        temps, cotangent, solid_mask, patch_ids,
        heat_coeff.reshape(64, CZ), owner_slot.reshape(64, CZ),
    )
    return sens, patch[0, :PATCH_PER]


def solution(mesh):
    placed = (
        P(None, "gx", "gy", "gz"),
        P("gx", "gy", "gz"),
        P("gx", "gy", "gz"),
        P("gx", "gy", "gz"),
        P(),
        P(),
    )
    return jax.shard_map(
        on_device,
        mesh=mesh,
        in_specs=placed,
        out_specs=(P("gx", "gy", "gz"), P(("gx", "gy", "gz"))),
        check_vma=False,
    )
```

```python
import jax
import jax.numpy as jnp
from jax import lax
from jax.experimental import pallas as pl
from jax.experimental.pallas import tpu as pltpu
from jax.sharding import PartitionSpec as P

STEPS = 3
PATCH_PER = 16
GX, GY, GZ = 16, 16, 2
CX, CY, CZ = 32, 16, 128
Y0 = 8
F32 = jnp.float32
MESH = pl.DeviceIdType.MESH

time_step = 0.12
ambient = 0.6


def x_loop(unroll, body, init):
    def block(i, carry):
        for k in range(unroll):
            carry = body(i * unroll + k, carry)
        return carry

    return lax.fori_loop(0, CX // unroll, block, init)


def sublane_sums(parts, sub):
    for width in (4, 2, 1):
        upper = (sub // width) % 2 == 1
        merged = []
        half = len(parts) // 2
        for low, high in zip(parts[:half], parts[half:]):
            low = low + pltpu.roll(low, 8 - width, 0)
            high = high + pltpu.roll(high, width, 0)
            merged.append(jnp.where(upper, high, low))
        parts = merged
    return parts[0]


def kernel(
    temps, cot, mask, ids, heat, owner,
    sens, patch,
    tpad, lpad, mpad, idv, heatv, ownv, hv, mm, kk, pe, tot,
    zsend, zrecv, arow, plane, rrow, zbuf,
    lsem, ssem, rsem, gsem, zsem,
):
    gx, gy, gz = lax.axis_index("gx"), lax.axis_index("gy"), lax.axis_index("gz")
    here = gx * GZ + gz

    def in_plane(r):
        j = lax.rem(here + r, GX * GZ)
        return (j // GZ, gy, lax.rem(j, GZ))

    def in_column(r):
        return (gx, lax.rem(gy + r + GY, GY), gz)

    x_up, x_down = (lax.rem(gx + 1, GX), gy, gz), (lax.rem(gx + GX - 1, GX), gy, gz)
    y_up, y_down = in_column(1), in_column(-1)
    z_other = (gx, gy, 1 - gz)

    barrier = pltpu.get_barrier_semaphore()
    for r in range(1, GX * GZ):
        pl.semaphore_signal(barrier, inc=1, device_id=in_plane(r), device_id_type=MESH)
    near = (1, -1, 2, -2, 3, -3, 4, -4)
    for r in near:
        pl.semaphore_signal(barrier, inc=1, device_id=in_column(r), device_id_type=MESH)

    inner = (pl.ds(1, CX), pl.ds(Y0, CY))
    loads = [
        (ids, idv), (heat, heatv), (owner, ownv), (mask, mpad.at[inner]),
        (cot, lpad.at[0].at[inner]),
        (temps.at[2], tpad.at[2].at[inner]),
        (temps.at[1], tpad.at[1].at[inner]),
        (temps.at[0], tpad.at[0].at[inner]),
    ]
    loads = [pltpu.make_async_copy(s, d, lsem.at[i]) for i, (s, d) in enumerate(loads)]
    for c in loads:
        c.start()
    for c in loads:
        c.wait()

    lane = lax.broadcasted_iota(jnp.int32, (CY, CZ), 1)
    row = lax.broadcasted_iota(jnp.int32, (CY, CZ), 0)
    lane8 = lax.broadcasted_iota(jnp.int32, (8, CZ), 1)
    sub8 = lax.broadcasted_iota(jnp.int32, (8, CZ), 0)
    edge = jnp.where(gz == 0, CZ - 1, 0)

    def to_lane(value, target):
        return pltpu.roll(value, lax.rem(target - edge + CZ, CZ), 1)

    def from_lane(packed, source):
        return pltpu.roll(packed, lax.rem(edge - source + CZ, CZ), 1)

    zero = jnp.zeros((CY, CZ), F32)

    def before(x, carry):
        first, second = carry
        a = lax.rem(gx + x // (CX // 2), GX)
        picked = []
        for half in range(2):
            b = lax.rem(gy + half, GY)
            table = jnp.broadcast_to(heatv[pl.ds(a * 4 + b // 4, 1), :], (8, CZ))
            index = jnp.bitwise_and(idv[x, half * 8 : half * 8 + 8, :], CZ - 1)
            picked.append(jnp.take_along_axis(table, index, axis=1))
        hv[x] = jnp.concatenate(picked, axis=0)
        ins = pl.ds(Y0, CY)
        first = jnp.where(lane == x, to_lane(lpad[0, x + 1, ins, :], x), first)
        first = jnp.where(lane == x + 32, to_lane(tpad[2, x + 1, ins, :], x + 32), first)
        first = jnp.where(lane == x + 64, to_lane(mpad[x + 1, ins, :].astype(F32), x + 64), first)
        second = jnp.where(lane == x, to_lane(tpad[1, x + 1, ins, :], x), second)
        second = jnp.where(lane == x + 32, to_lane(tpad[0, x + 1, ins, :], x + 32), second)
        return first, second

    first, second = x_loop(4, before, (zero, zero))
    zsend[0] = first
    zsend[1] = second

    b0, b1 = gy, lax.rem(gy + 1, GY)
    s0 = ownv[pl.ds(b0 // 4, GX, stride=4), :]
    s1 = ownv[pl.ds(b1 // 4, GX, stride=4), :]
    s0 = pltpu.roll(s0, lax.rem(CZ - lax.rem(b0, 4) * 32, CZ), 1)
    s1 = pltpu.roll(s1, lax.rem(CZ + 32 - lax.rem(b1, 4) * 32, CZ), 1)
    s16 = jnp.where(lane < 32, s0, s1)
    slots = jnp.where(lane8 < 64, s16[:8], pltpu.roll(s16[8:], 64, 1))

    pl.semaphore_wait(barrier, GX * GZ - 1 + len(near))

    counter = [0]

    def remote(src, dst, device):
        i = counter[0]
        counter[0] += 1
        copy = pltpu.make_async_remote_copy(
            src_ref=src, dst_ref=dst, send_sem=ssem.at[i], recv_sem=rsem.at[i],
            device_id=device, device_id_type=MESH,
        )
        copy.start()
        return copy

    def x_faces(ref):
        ins = pl.ds(Y0, CY)
        return [
            remote(ref.at[CX, ins], ref.at[0, ins], x_up),
            remote(ref.at[1, ins], ref.at[CX + 1, ins], x_down),
        ]

    def y_faces(ref):
        ins = pl.ds(1, CX)
        return [
            remote(ref.at[ins, pl.ds(Y0 + CY - 1, 1)], ref.at[ins, pl.ds(Y0 - 1, 1)], y_up),
            remote(ref.at[ins, pl.ds(Y0, 1)], ref.at[ins, pl.ds(Y0 + CY, 1)], y_down),
        ]

    def z_face(i):
        return [remote(zsend.at[i], zrecv.at[i], z_other)]

    sent = []

    def landed(copies):
        sent.extend(copies)
        for c in copies:
            c.wait_recv()

    head = [mpad, lpad.at[0], tpad.at[2]]
    round_1 = sum([x_faces(r) for r in head], []) + z_face(0) + sum([y_faces(r) for r in head], [])
    tail = [tpad.at[1], tpad.at[0]]
    later_1 = [x_faces(tail[0]) + y_faces(tail[0]) + z_face(1), x_faces(tail[1]) + y_faces(tail[1])]
    for r in (4, -4):
        pl.semaphore_signal(zsem, inc=1, device_id=in_column(r), device_id_type=MESH)
    landed(round_1)

    def z_neighbours(value, halo):
        up = jnp.where(lane == CZ - 1, halo, pltpu.roll(value, CZ - 1, 1))
        down = jnp.where(lane == 0, halo, pltpu.roll(value, 1, 1))
        return up, down

    def six(ref, x, halo):
        ins = pl.ds(Y0, CY)
        here = ref[x + 1, ins, :]
        up, down = z_neighbours(here, halo)
        return here, [
            ref[x + 2, ins, :], ref[x, ins, :],
            ref[x + 1, pl.ds(Y0 + 1, CY), :], ref[x + 1, pl.ds(Y0 - 1, CY), :],
            up, down,
        ]

    inside = lambda cond: jnp.where(cond, 1.0, 0.0).astype(F32)
    keep_y_up = jnp.where(row == CY - 1, inside(gy < GY - 1), 1.0)
    keep_y_down = jnp.where(row == 0, inside(gy > 0), 1.0)
    keep_z_up = jnp.where(lane == CZ - 1, inside(gz == 0), 1.0)
    keep_z_down = jnp.where(lane == 0, inside(gz == 1), 1.0)

    def masks(x):
        halo = from_lane(zrecv[0], x + 64)
        ins = pl.ds(Y0, CY)
        centre = mpad[x + 1, ins, :].astype(F32)
        up, down = z_neighbours(centre, halo)
        others = [
            mpad[x + 2, ins, :].astype(F32) * inside((x < CX - 1) | (gx < GX - 1)),
            mpad[x, ins, :].astype(F32) * inside((x > 0) | (gx > 0)),
            mpad[x + 1, pl.ds(Y0 + 1, CY), :].astype(F32) * keep_y_up,
            mpad[x + 1, pl.ds(Y0 - 1, CY), :].astype(F32) * keep_y_down,
            up * keep_z_up,
            down * keep_z_down,
        ]
        active = others[0]
        for m in others[1:]:
            active = active + m
        scaled = time_step * centre
        surface = scaled * (6.0 - active)
        pe[x] = surface
        faces = [scaled * m for m in others]
        for d in range(6):
            mm[d, x] = faces[d]
        return faces, surface

    def coefficients(level, x, halo, faces, surface):
        here, there = six(tpad.at[level], x, halo)
        base = 1.0 + 0.75 * (here * here)
        half = 0.5 * here
        centre = 1.0 - surface * hv[x]
        out = []
        for t, m in zip(there, faces):
            k = m * (base + t * (0.25 * t - half))
            centre = centre - k
            out.append(k)
        return out, centre, here

    def apply(number, x, halo, out, centre):
        here, there = six(lpad.at[number], x, halo)
        new = centre * here
        for k, l in zip(out, there):
            new = new + k * l
        return new, here

    def step_1(x, packed):
        faces, surface = masks(x)
        out, centre, t = coefficients(2, x, from_lane(zrecv[0], x + 32), faces, surface)
        new, old = apply(0, x, from_lane(zrecv[0], x), out, centre)
        tot[x] = (t - ambient) * old
        lpad[1, x + 1, pl.ds(Y0, CY), :] = new
        return jnp.where(lane == x, to_lane(new, x), packed)

    zsend[2] = x_loop(4, step_1, zero)
    round_2 = x_faces(lpad.at[1]) + y_faces(lpad.at[1]) + z_face(2)

    def prepare(level, source):
        def body(x, carry):
            faces = [mm[d, x] for d in range(6)]
            out, centre, t = coefficients(level, x, from_lane(zrecv[1], x + source), faces, pe[x])
            for d in range(6):
                kk[d, x] = out[d]
            kk[6, x] = centre
            tot[x] = tot[x] + (t - ambient) * lpad[2 - level, x + 1, pl.ds(Y0, CY), :]
            return carry

        x_loop(4, body, 0)

    landed(later_1[0])
    prepare(1, 0)
    landed(round_2)

    def step_2(x, packed):
        new, _ = apply(1, x, from_lane(zrecv[2], x), [kk[d, x] for d in range(6)], kk[6, x])
        lpad[2, x + 1, pl.ds(Y0, CY), :] = new
        t0 = tpad[0, x + 1, pl.ds(Y0, CY), :]
        tot[x] = -pe[x] * (tot[x] + (t0 - ambient) * new)
        return jnp.where(lane == x, to_lane(new, x), packed)

    zsend[3] = x_loop(4, step_2, zero)

    by_depth = [jnp.where(lane8 // (CZ // 2) == (gz if c == 0 else 1 - gz), 1.0, 0.0) for c in range(2)]
    rows = []
    for xh in range(2):
        def gather(i, accs):
            for k in range(2):
                x = xh * (CX // 2) + 2 * i + k
                value = tot[x]
                offset = jnp.bitwise_and(idv[x], PATCH_PER - 1)
                accs = [acc + jnp.where(offset == o, value, 0.0) for o, acc in enumerate(accs)]
            return accs

        accs = lax.fori_loop(0, CX // 4, gather, [zero] * PATCH_PER)
        for yh in range(2):
            parts = [a[yh * 8 : yh * 8 + 8] for a in accs]
            low, high = sublane_sums(parts[:8], sub8), sublane_sums(parts[8:], sub8)
            for c in range(2):
                rows += [low * by_depth[c], high * by_depth[c]]
    rows = jnp.concatenate(rows, axis=0)
    across = (((1,), (1,)), ((), ()))
    message = lax.dot_general(
        jnp.ones((8, CZ), F32), rows, across,
        precision=lax.Precision.HIGHEST, preferred_element_type=F32,
    )
    arow[...] = message

    own_row = gz * GX + gx
    for r in range(1, GX * GZ):
        pltpu.make_async_remote_copy(
            src_ref=arow.at[pl.ds(0, 1)], dst_ref=plane.at[pl.ds(own_row, 1)],
            send_sem=gsem.at[0], recv_sem=gsem.at[1],
            device_id=in_plane(r), device_id_type=MESH,
        ).start()
    round_3 = x_faces(lpad.at[2]) + y_faces(lpad.at[2]) + z_face(3)
    landed(later_1[1])
    prepare_0 = lambda x: coefficients(
        0, x, from_lane(zrecv[1], x + 32), [mm[d, x] for d in range(6)], pe[x]
    )

    count = pl.ds(0, GX * GZ - 1)
    pltpu.make_async_copy(plane.at[count], plane.at[count], gsem.at[1]).wait()
    row32 = lax.broadcasted_iota(jnp.int32, (GX * GZ, CZ), 0)
    sums = jnp.where(row32 == own_row, message[:1], plane[...])
    sums = sums[:GX] + sums[GX:]
    shifted = pltpu.roll(sums, 64, 1)
    sums = sums + jnp.concatenate([shifted[GX - 1 :], shifted[: GX - 1]], axis=0)
    sums = jnp.where(lane8 < 64, sums[:8], pltpu.roll(sums[8:], 64, 1))

    mine = jnp.where((slots // 512 == gx) & (lax.rem(slots // 16, 2) == gz), sums, 0.0)
    target = lax.rem(slots // 32, GY)
    place = lax.rem(slots, PATCH_PER)
    values, marks = [], []
    for r in range(8):
        values.append(jnp.where(target[r : r + 1] == row, mine[r : r + 1], 0.0))
        marks.append(jnp.where(place[r : r + 1] == row, 1.0, 0.0))
    share = lax.dot_general(
        jnp.concatenate(values, axis=1),
        jnp.concatenate([jnp.concatenate([m, jnp.zeros((CZ - GY, CZ), F32)], axis=0) for m in marks], axis=1),
        across, precision=lax.Precision.HIGHEST, preferred_element_type=F32,
    )
    rrow[...] = share
    pl.semaphore_wait(zsem, 2)
    for r in range(1, GY):
        to = in_column(r)
        pltpu.make_async_remote_copy(
            src_ref=rrow.at[pl.ds(to[1], 1)], dst_ref=zbuf.at[pl.ds(gy, 1)],
            send_sem=gsem.at[2], recv_sem=gsem.at[3],
            device_id=to, device_id_type=MESH,
        ).start()

    landed(round_3)

    def step_3(x, carry):
        out, centre, _ = prepare_0(x)
        new, _ = apply(2, x, from_lane(zrecv[3], x), out, centre)
        sens[x] = new
        return carry

    x_loop(4, step_3, 0)
    for c in sent:
        c.wait_send()
    pltpu.make_async_copy(plane.at[count], plane.at[count], gsem.at[0]).wait()
    count = pl.ds(0, GY - 1)
    pltpu.make_async_copy(zbuf.at[count], zbuf.at[count], gsem.at[3]).wait()
    final = jnp.where(row == gy, share, zbuf[...])
    patch[...] = jnp.sum(final, axis=0)[:PATCH_PER]
    pltpu.make_async_copy(zbuf.at[count], zbuf.at[count], gsem.at[2]).wait()


def on_device(temps, cotangent, solid_mask, patch_ids, heat_coeff, owner_slot):
    anywhere = pl.BlockSpec(memory_space=pltpu.HBM)
    vmem = pl.BlockSpec(memory_space=pltpu.VMEM)
    field = (CX, CY, CZ)
    copies = 12 + 2 + 4 * 2 + 2 * 5
    sens, patch = pl.pallas_call(
        kernel,
        name="adjoint",
        out_shape=(
            pltpu.VMEM(field, F32),
            pltpu.VMEM((PATCH_PER,), F32),
        ),
        in_specs=[anywhere] * 6,
        out_specs=(vmem, vmem),
        scratch_shapes=[
            pltpu.VMEM((3, CX + 2, CY + 16, CZ), F32),
            pltpu.VMEM((3, CX + 2, CY + 16, CZ), F32),
            pltpu.VMEM((CX + 2, CY + 16, CZ), jnp.int32),
            pltpu.VMEM(field, jnp.int32),
            pltpu.VMEM((64, CZ), F32),
            pltpu.VMEM((64, CZ), jnp.int32),
            pltpu.VMEM(field, F32),
            pltpu.VMEM((6,) + field, F32),
            pltpu.VMEM((7,) + field, F32),
            pltpu.VMEM(field, F32),
            pltpu.VMEM(field, F32),
            pltpu.VMEM((4, CY, CZ), F32),
            pltpu.VMEM((4, CY, CZ), F32),
            pltpu.VMEM((8, CZ), F32),
            pltpu.VMEM((GX * GZ, CZ), F32),
            pltpu.VMEM((GY, CZ), F32),
            pltpu.VMEM((GY, CZ), F32),
            pltpu.SemaphoreType.DMA((8,)),
            pltpu.SemaphoreType.DMA((copies,)),
            pltpu.SemaphoreType.DMA((copies,)),
            pltpu.SemaphoreType.DMA((4,)),
            pltpu.SemaphoreType.REGULAR,
        ],
        compiler_params=pltpu.CompilerParams(
            collective_id=0, has_side_effects=True, vmem_limit_bytes=60 * 1024 * 1024
        ),
    )(
        temps, cotangent, solid_mask, patch_ids,
        heat_coeff.reshape(64, CZ), owner_slot.reshape(64, CZ),
    )
    return sens, patch


def solution(mesh):
    placed = (
        P(None, "gx", "gy", "gz"),
        P("gx", "gy", "gz"),
        P("gx", "gy", "gz"),
        P("gx", "gy", "gz"),
        P(),
        P(),
    )
    return jax.shard_map(
        on_device,
        mesh=mesh,
        in_specs=placed,
        out_specs=(P("gx", "gy", "gz"), P(("gx", "gy", "gz"))),
        check_vma=False,
    )
```

```python
import jax
import jax.numpy as jnp
from jax import lax
from jax.experimental import pallas as pl
from jax.experimental.pallas import tpu as pltpu
from jax.sharding import PartitionSpec as P

STEPS = 3
PATCH_PER = 16
GX, GY, GZ = 16, 16, 2
CX, CY, CZ = 32, 16, 128
Y0 = 8
F32 = jnp.float32
MESH = pl.DeviceIdType.MESH

time_step = 0.12
ambient = 0.6


def x_loop(unroll, body, init):
    def block(i, carry):
        stores = []
        for k in range(unroll):
            carry = body(i * unroll + k, carry, lambda *store: stores.append(store))
        for ref, index, value in stores:
            ref[index] = value
        return carry

    return lax.fori_loop(0, CX // unroll, block, init)


def sublane_sums(parts, sub):
    for width in (4, 2, 1):
        upper = (sub // width) % 2 == 1
        merged = []
        half = len(parts) // 2
        for low, high in zip(parts[:half], parts[half:]):
            low = low + pltpu.roll(low, 8 - width, 0)
            high = high + pltpu.roll(high, width, 0)
            merged.append(jnp.where(upper, high, low))
        parts = merged
    return parts[0]


MASK, LAM, TEMP, PART, HEAT = range(5)


def kernel(
    temps, cot, mask, ids, heat, owner,
    sens, patch,
    comb, tpad, l2, lpad, mraw, idv, heatv, ownv, hv, mm, pe, tot,
    ysend, yrecv, corner, ycor, l2y, xcor,
    zsend, zrecv, zx, zy, zwork, arow, plane, rrow, zbuf,
    lsem, ssem, rsem, gsem, zsem,
):
    gx, gy, gz = lax.axis_index("gx"), lax.axis_index("gy"), lax.axis_index("gz")
    here = gx * GZ + gz

    def in_plane(r):
        j = lax.rem(here + r, GX * GZ)
        return (j // GZ, gy, lax.rem(j, GZ))

    def at(dx, dy, dz):
        return (lax.rem(gx + dx + GX, GX), lax.rem(gy + dy + GY, GY), 1 - gz if dz else gz)

    def in_column(r):
        return at(0, r, 0)

    barrier = pltpu.get_barrier_semaphore()
    near = [in_plane(r) for r in range(1, GX * GZ)]
    near += [in_column(r) for r in (1, -1, 2, -2, 3, -3, 4, -4)]
    near += [at(dx, dy, 0) for dx in (1, -1) for dy in (1, -1)]
    near += [at(0, dy, 1) for dy in (1, -1)]
    for device in near:
        pl.semaphore_signal(barrier, inc=1, device_id=device, device_id_type=MESH)

    inner = (pl.ds(1, CX), pl.ds(Y0, CY))
    loads = [
        (mask, mraw), (cot, comb.at[LAM, pl.ds(1, CX)]), (temps.at[2], comb.at[TEMP, pl.ds(1, CX)]),
        (ids, idv), (heat, heatv), (owner, ownv),
        (temps.at[1], tpad.at[1].at[inner]),
        (temps.at[0], tpad.at[0].at[inner]),
    ]
    loads = [pltpu.make_async_copy(s, d, lsem.at[i]) for i, (s, d) in enumerate(loads)]
    for c in loads:
        c.start()
    for c in loads:
        c.wait()

    lane = lax.broadcasted_iota(jnp.int32, (CY, CZ), 1)
    row = lax.broadcasted_iota(jnp.int32, (CY, CZ), 0)
    lane8 = lax.broadcasted_iota(jnp.int32, (8, CZ), 1)
    sub8 = lax.broadcasted_iota(jnp.int32, (8, CZ), 0)
    lane32 = lax.broadcasted_iota(jnp.int32, (CX, CZ), 1)
    row32 = lax.broadcasted_iota(jnp.int32, (CX, CZ), 0)
    edge = jnp.where(gz == 0, CZ - 1, 0)
    ins = pl.ds(Y0, CY)

    def to_lane(value, target):
        return pltpu.roll(value, lax.rem(target - edge + CZ, CZ), 1)

    def from_lane(packed, source):
        return pltpu.roll(packed, lax.rem(edge - source + CZ, CZ), 1)

    def contribution(one, other):
        m, l, t, hl = one
        mo, lo, to = other
        g = 1.0 + 0.75 * (t * t) + to * (0.25 * to - 0.5 * t)
        return time_step * (m * mo) * (g * (lo - l) + hl)

    mraw_f = lambda x: mraw[x].astype(F32)

    def convert(x, carry, put):
        put(comb, (MASK, x + 1), mraw_f(x))
        return carry

    x_loop(8, convert, 0)
    zero = jnp.zeros((CY, CZ), F32)
    inside = lambda cond: jnp.where(cond, 1.0, 0.0).astype(F32)
    own_up_y, own_down_y = inside(row < CY - 1), inside(row > 0)
    own_up_z, own_down_z = inside(lane < CZ - 1), inside(lane > 0)

    def around(value):
        return (
            pltpu.roll(value, CY - 1, 0), pltpu.roll(value, 1, 0),
            pltpu.roll(value, CZ - 1, 1), pltpu.roll(value, 1, 1),
        )

    def before(x, carry, put):
        first, second = carry
        a = lax.rem(gx + x // (CX // 2), GX)
        picked = []
        for half in range(2):
            b = lax.rem(gy + half, GY)
            table = jnp.broadcast_to(heatv[pl.ds(a * 4 + b // 4, 1), :], (8, CZ))
            index = jnp.bitwise_and(idv[x, half * 8 : half * 8 + 8, :], CZ - 1)
            picked.append(jnp.take_along_axis(table, index, axis=1))
        h = jnp.concatenate(picked, axis=0)
        put(hv, x, h)
        m, l, t = comb[MASK, x + 1], comb[LAM, x + 1], comb[TEMP, x + 1]
        hl = h * l
        above, below = jnp.minimum(x + 2, CX), jnp.maximum(x, 1)
        ms = (comb[MASK, above] * inside(x < CX - 1), comb[MASK, below] * inside(x > 0))
        my = around(m)
        ms += (my[0] * own_up_y, my[1] * own_down_y, my[2] * own_up_z, my[3] * own_down_z)
        ls = (comb[LAM, above], comb[LAM, below]) + around(l)
        ts = (comb[TEMP, above], comb[TEMP, below]) + around(t)
        base, half_t = 1.0 + 0.75 * (t * t), 0.5 * t
        added = -6.0 * hl
        for mo, lo, to in zip(ms, ls, ts):
            added = added + mo * ((base + to * (0.25 * to - half_t)) * (lo - l) + hl)
        part = l + (time_step * m) * added
        put(comb, (PART, x + 1), part)
        put(comb, (HEAT, x + 1), hl)
        put(tot, x, (t - ambient) * l)
        for f, value in enumerate((m, l, t, part, hl)):
            put(ysend, (0, f, pl.ds(x, 1), slice(None)), value[:1])
            put(ysend, (1, f, pl.ds(x, 1), slice(None)), value[CY - 1 :])
        for f, value in enumerate((m, l, t, part)):
            first = jnp.where(lane == x + 32 * f, to_lane(value, x + 32 * f), first)
        for f, value in enumerate((hl, tpad[1, x + 1, ins, :], tpad[0, x + 1, ins, :])):
            second = jnp.where(lane == x + 32 * f, to_lane(value, x + 32 * f), second)
        return first, second

    first, second = x_loop(4, before, (zero, zero))
    zsend[0] = first
    zsend[1] = second

    b0, b1 = gy, lax.rem(gy + 1, GY)
    s0 = ownv[pl.ds(b0 // 4, GX, stride=4), :]
    s1 = ownv[pl.ds(b1 // 4, GX, stride=4), :]
    s0 = pltpu.roll(s0, lax.rem(CZ - lax.rem(b0, 4) * 32, CZ), 1)
    s1 = pltpu.roll(s1, lax.rem(CZ + 32 - lax.rem(b1, 4) * 32, CZ), 1)
    s16 = jnp.where(lane < 32, s0, s1)
    slots = jnp.where(lane8 < 64, s16[:8], pltpu.roll(s16[8:], 64, 1))

    pl.semaphore_wait(barrier, len(near))

    counter = [0]

    def remote(src, dst, device):
        i = counter[0]
        counter[0] += 1
        copy = pltpu.make_async_remote_copy(
            src_ref=src, dst_ref=dst, send_sem=ssem.at[i], recv_sem=rsem.at[i],
            device_id=device, device_id_type=MESH,
        )
        copy.start()
        return copy

    def x_faces(ref):
        return [
            remote(ref.at[CX, ins], ref.at[0, ins], at(1, 0, 0)),
            remote(ref.at[1, ins], ref.at[CX + 1, ins], at(-1, 0, 0)),
        ]

    def y_faces(ref):
        xs = pl.ds(1, CX)
        return [
            remote(ref.at[xs, pl.ds(Y0 + CY - 1, 1)], ref.at[xs, pl.ds(Y0 - 1, 1)], at(0, 1, 0)),
            remote(ref.at[xs, pl.ds(Y0, 1)], ref.at[xs, pl.ds(Y0 + CY, 1)], at(0, -1, 0)),
        ]

    sent = []

    def landed(copies):
        sent.extend(copies)
        for c in copies:
            c.wait_recv()

    three = pl.ds(0, 3)
    round_1 = []
    for s, dx in ((0, 1), (1, -1)):
        for t, dy in ((0, 1), (1, -1)):
            x, y = (CX - 1 if dx == 1 else 0), (1 if dy == 1 else 0)
            round_1.append(remote(
                ysend.at[y, three, pl.ds(x, 1)], corner.at[s, t, three, pl.ds(0, 1)], at(dx, dy, 0)
            ))
    round_1 += [
        remote(comb.at[:, CX], comb.at[:, 0], at(1, 0, 0)),
        remote(comb.at[:, 1], comb.at[:, CX + 1], at(-1, 0, 0)),
        remote(zsend.at[0], zx.at[0], at(1, 0, 1)),
        remote(zsend.at[0], zx.at[1], at(-1, 0, 1)),
        remote(zsend.at[0], zy.at[0], at(0, 1, 1)),
        remote(zsend.at[0], zy.at[1], at(0, -1, 1)),
        remote(zsend.at[pl.ds(0, 2)], zrecv.at[pl.ds(0, 2)], at(0, 0, 1)),
        remote(ysend.at[1], yrecv.at[0], at(0, 1, 0)),
        remote(ysend.at[0], yrecv.at[1], at(0, -1, 0)),
    ]
    later_1 = [x_faces(tpad.at[i]) + y_faces(tpad.at[i]) for i in (1, 0)]
    for r in (4, -4):
        pl.semaphore_signal(zsem, inc=1, device_id=in_column(r), device_id_type=MESH)
    landed(round_1)

    keep_x = (inside(gx > 0), inside(gx < GX - 1))
    keep_y = (inside(gy > 0), inside(gy < GY - 1))
    first_row, last_row = row == 0, row == CY - 1
    at_edge = inside(lane == edge)

    for s in range(2):
        mine, outer = (1, 0) if s == 0 else (CX, CX + 1)
        o = [comb[f, mine] for f in (MASK, LAM, TEMP, HEAT)]
        v = [comb[f, outer] for f in (MASK, LAM, TEMP, HEAT)]
        v[0] = v[0] * keep_x[s]
        xcor[s] = contribution(o, v[:3])
        new = comb[PART, outer] + contribution(v, o[:3])
        w = [jnp.where(first_row, corner[s, 0, f, :1, :], corner[s, 1, f, :1, :]) for f in range(3)]
        w[0] = w[0] * jnp.where(first_row, keep_y[0], jnp.where(last_row, keep_y[1], 0.0))
        new = new + contribution(v, w)
        source = CX - 1 if s == 0 else 0
        w = [from_lane(zx[s], 32 * f + source) for f in range(3)]
        w[0] = w[0] * at_edge
        l2[outer] = new + contribution(v, w)

    first_x, last_x = row32 == 0, row32 == CX - 1
    at_edge32 = inside(lane32 == edge)
    for t in range(2):
        o = [ysend[t, f] for f in (MASK, LAM, TEMP, HEAT)]
        v = [yrecv[t, f] for f in (MASK, LAM, TEMP, HEAT)]
        v[0] = v[0] * keep_y[t]
        ycor[t] = contribution(o, v[:3])
        new = yrecv[t, PART] + contribution(v, o[:3])
        w = [jnp.where(first_x, corner[0, t, f, :1, :], corner[1, t, f, :1, :]) for f in range(3)]
        w[0] = w[0] * jnp.where(first_x, keep_x[0], jnp.where(last_x, keep_x[1], 0.0))
        new = new + contribution(v, w)
        line = jnp.broadcast_to(zy[t, CY - 1 :, :] if t == 0 else zy[t, :1, :], (CX, CZ))
        w = [
            jnp.sum(jnp.where(lane32 == row32 + 32 * f, line, 0.0), axis=1, keepdims=True)
            for f in range(3)
        ]
        w = [jnp.broadcast_to(c, (CX, CZ)) for c in w]
        w[0] = w[0] * at_edge32
        l2y[t] = new + contribution(v, w)

    def group(packed, f):
        return packed if f == 0 else pltpu.roll(packed, CZ - 32 * f, 1)

    def moved(packed, source, target):
        shift = (target - source) % CZ
        return packed if shift == 0 else pltpu.roll(packed, shift, 1)

    o = [group(zsend[0], f) for f in range(3)] + [zsend[1]]
    v = [group(zrecv[0], f) for f in range(3)] + [zrecv[1]]
    zwork[0] = contribution(o, v[:3])
    new = group(zrecv[0], 3) + contribution(v, o[:3])
    w = [
        jnp.where(lane == 0, moved(zx[0], 32 * f + CX - 1, 0), moved(zx[1], 32 * f, CX - 1))
        for f in range(3)
    ]
    w[0] = w[0] * jnp.where(lane == 0, keep_x[0], jnp.where(lane == CX - 1, keep_x[1], 0.0))
    new = new + contribution(v, w)
    w = [
        jnp.where(first_row, group(zy[0, CY - 1 :, :], f), group(zy[1, :1, :], f))
        for f in range(3)
    ]
    w[0] = w[0] * jnp.where(first_row, keep_y[0], jnp.where(last_row, keep_y[1], 0.0))
    zwork[1] = new + contribution(v, w)

    def finish_1(x, carry, put):
        new = comb[PART, x + 1] + from_lane(zwork[0], x) * at_edge
        new = new + jnp.where(first_row, ycor[0, pl.ds(x, 1), :], 0.0)
        put(l2, x + 1, new + jnp.where(last_row, ycor[1, pl.ds(x, 1), :], 0.0))
        return carry

    x_loop(8, finish_1, 0)
    l2[1] = l2[1] + xcor[0]
    l2[CX] = l2[CX] + xcor[1]

    def z_neighbours(value, halo):
        up = jnp.where(lane == CZ - 1, halo, pltpu.roll(value, CZ - 1, 1))
        down = jnp.where(lane == 0, halo, pltpu.roll(value, 1, 1))
        return [up, down]

    def y_neighbours(value, up, down):
        return [
            jnp.where(last_row, up, pltpu.roll(value, CY - 1, 0)),
            jnp.where(first_row, down, pltpu.roll(value, 1, 0)),
        ]

    def six(ref, x, halo):
        here = ref[x + 1, ins, :]
        return here, [
            ref[x + 2, ins, :], ref[x, ins, :],
            ref[x + 1, pl.ds(Y0 + 1, CY), :], ref[x + 1, pl.ds(Y0 - 1, CY), :],
        ] + z_neighbours(here, halo)

    def masks(x, put):
        centre = comb[MASK, x + 1]
        up, down = z_neighbours(centre, from_lane(zrecv[0], x))
        others = [
            comb[MASK, x + 2] * inside((x < CX - 1) | (gx < GX - 1)),
            comb[MASK, x] * inside((x > 0) | (gx > 0)),
        ]
        others += y_neighbours(
            centre, yrecv[1, MASK, pl.ds(x, 1), :] * keep_y[1], yrecv[0, MASK, pl.ds(x, 1), :] * keep_y[0]
        )
        others += [
            up * jnp.where(lane == CZ - 1, inside(gz == 0), 1.0),
            down * jnp.where(lane == 0, inside(gz == 1), 1.0),
        ]
        active = others[0]
        for m in others[1:]:
            active = active + m
        scaled = time_step * centre
        surface = scaled * (6.0 - active)
        put(pe, x, surface)
        faces = [scaled * m for m in others]
        for d in range(6):
            put(mm, (d, x), faces[d])
        return faces, surface

    def coefficients(level, x, halo, faces, surface):
        here, there = six(tpad.at[level], x, halo)
        base = 1.0 + 0.75 * (here * here)
        half = 0.5 * here
        centre = 1.0 - surface * hv[x]
        out = []
        for t, m in zip(there, faces):
            k = m * (base + t * (0.25 * t - half))
            centre = centre - k
            out.append(k)
        return out, centre, here

    def apply(here, there, out, centre):
        new = centre * here
        for k, l in zip(out, there):
            new = new + k * l
        return new

    landed(later_1[0])

    def step_2(x, packed, put):
        faces, surface = masks(x, put)
        out, centre, t1 = coefficients(1, x, from_lane(zrecv[1], x + 32), faces, surface)
        here = l2[x + 1]
        there = [l2[x + 2], l2[x]]
        there += y_neighbours(here, l2y[1, pl.ds(x, 1), :], l2y[0, pl.ds(x, 1), :])
        there += z_neighbours(here, from_lane(zwork[1], x))
        new = apply(here, there, out, centre)
        put(lpad, (x + 1, ins, slice(None)), new)
        t0 = tpad[0, x + 1, ins, :]
        put(tot, x, -surface * (tot[x] + (t1 - ambient) * here + (t0 - ambient) * new))
        return jnp.where(lane == x, to_lane(new, x), packed)

    zsend[2] = x_loop(8, step_2, zero)

    by_depth = [jnp.where(lane8 // (CZ // 2) == (gz if c == 0 else 1 - gz), 1.0, 0.0) for c in range(2)]
    rows = []
    for xh in range(2):
        def gather(i, accs):
            for k in range(2):
                x = xh * (CX // 2) + 2 * i + k
                value = tot[x]
                offset = jnp.bitwise_and(idv[x], PATCH_PER - 1)
                accs = [acc + jnp.where(offset == o, value, 0.0) for o, acc in enumerate(accs)]
            return accs

        accs = lax.fori_loop(0, CX // 4, gather, [zero] * PATCH_PER)
        for yh in range(2):
            parts = [a[yh * 8 : yh * 8 + 8] for a in accs]
            low, high = sublane_sums(parts[:8], sub8), sublane_sums(parts[8:], sub8)
            for c in range(2):
                rows += [low * by_depth[c], high * by_depth[c]]
    rows = jnp.concatenate(rows, axis=0)
    across = (((1,), (1,)), ((), ()))
    message = lax.dot_general(
        jnp.ones((8, CZ), F32), rows, across,
        precision=lax.Precision.HIGHEST, preferred_element_type=F32,
    )
    arow[...] = message

    own_row = gz * GX + gx
    for r in range(1, GX * GZ):
        pltpu.make_async_remote_copy(
            src_ref=arow.at[pl.ds(0, 1)], dst_ref=plane.at[pl.ds(own_row, 1)],
            send_sem=gsem.at[0], recv_sem=gsem.at[1],
            device_id=in_plane(r), device_id_type=MESH,
        ).start()
    round_3 = x_faces(lpad) + y_faces(lpad) + [remote(zsend.at[2], zrecv.at[2], at(0, 0, 1))]
    landed(later_1[1])
    prepare_0 = lambda x: coefficients(
        0, x, from_lane(zrecv[1], x + 64), [mm[d, x] for d in range(6)], pe[x]
    )

    count = pl.ds(0, GX * GZ - 1)
    pltpu.make_async_copy(plane.at[count], plane.at[count], gsem.at[1]).wait()
    sums = jnp.where(row32 == own_row, message[:1], plane[...])
    sums = sums[:GX] + sums[GX:]
    shifted = pltpu.roll(sums, 64, 1)
    sums = sums + jnp.concatenate([shifted[GX - 1 :], shifted[: GX - 1]], axis=0)
    sums = jnp.where(lane8 < 64, sums[:8], pltpu.roll(sums[8:], 64, 1))

    mine = jnp.where((slots // 512 == gx) & (lax.rem(slots // 16, 2) == gz), sums, 0.0)
    target = lax.rem(slots // 32, GY)
    place = lax.rem(slots, PATCH_PER)
    values, marks = [], []
    for r in range(8):
        values.append(jnp.where(target[r : r + 1] == row, mine[r : r + 1], 0.0))
        marks.append(jnp.where(place[r : r + 1] == row, 1.0, 0.0))
    share = lax.dot_general(
        jnp.concatenate(values, axis=1),
        jnp.concatenate([jnp.concatenate([m, jnp.zeros((CZ - GY, CZ), F32)], axis=0) for m in marks], axis=1),
        across, precision=lax.Precision.HIGHEST, preferred_element_type=F32,
    )
    rrow[...] = share
    pl.semaphore_wait(zsem, 2)
    for r in range(1, GY):
        to = in_column(r)
        pltpu.make_async_remote_copy(
            src_ref=rrow.at[pl.ds(to[1], 1)], dst_ref=zbuf.at[pl.ds(gy, 1)],
            send_sem=gsem.at[2], recv_sem=gsem.at[3],
            device_id=to, device_id_type=MESH,
        ).start()

    landed(round_3)

    def step_3(x, carry, put):
        out, centre, _ = prepare_0(x)
        here, there = six(lpad, x, from_lane(zrecv[2], x))
        put(sens, x, apply(here, there, out, centre))
        return carry

    x_loop(4, step_3, 0)
    for c in sent:
        c.wait_send()
    pltpu.make_async_copy(plane.at[count], plane.at[count], gsem.at[0]).wait()
    count = pl.ds(0, GY - 1)
    pltpu.make_async_copy(zbuf.at[count], zbuf.at[count], gsem.at[3]).wait()
    final = jnp.where(row == gy, share, zbuf[...])
    patch[...] = jnp.sum(final, axis=0)[:PATCH_PER]
    pltpu.make_async_copy(zbuf.at[count], zbuf.at[count], gsem.at[2]).wait()


def on_device(temps, cotangent, solid_mask, patch_ids, heat_coeff, owner_slot):
    anywhere = pl.BlockSpec(memory_space=pltpu.HBM)
    vmem = pl.BlockSpec(memory_space=pltpu.VMEM)
    field = (CX, CY, CZ)
    copies = 13 + 4 * 2 + 5
    sens, patch = pl.pallas_call(
        kernel,
        name="adjoint",
        out_shape=(
            pltpu.VMEM(field, F32),
            pltpu.VMEM((PATCH_PER,), F32),
        ),
        in_specs=[anywhere] * 6,
        out_specs=(vmem, vmem),
        scratch_shapes=[
            pltpu.VMEM((5, CX + 2, CY, CZ), F32),
            pltpu.VMEM((2, CX + 2, CY + 16, CZ), F32),
            pltpu.VMEM((CX + 2, CY, CZ), F32),
            pltpu.VMEM((CX + 2, CY + 16, CZ), F32),
            pltpu.VMEM(field, jnp.int32),
            pltpu.VMEM(field, jnp.int32),
            pltpu.VMEM((64, CZ), F32),
            pltpu.VMEM((64, CZ), jnp.int32),
            pltpu.VMEM(field, F32),
            pltpu.VMEM((6,) + field, F32),
            pltpu.VMEM(field, F32),
            pltpu.VMEM(field, F32),
            pltpu.VMEM((2, 5, CX, CZ), F32),
            pltpu.VMEM((2, 5, CX, CZ), F32),
            pltpu.VMEM((2, 2, 3, 8, CZ), F32),
            pltpu.VMEM((2, CX, CZ), F32),
            pltpu.VMEM((2, CX, CZ), F32),
            pltpu.VMEM((2, CY, CZ), F32),
            pltpu.VMEM((3, CY, CZ), F32),
            pltpu.VMEM((3, CY, CZ), F32),
            pltpu.VMEM((2, CY, CZ), F32),
            pltpu.VMEM((2, CY, CZ), F32),
            pltpu.VMEM((2, CY, CZ), F32),
            pltpu.VMEM((8, CZ), F32),
            pltpu.VMEM((GX * GZ, CZ), F32),
            pltpu.VMEM((GY, CZ), F32),
            pltpu.VMEM((GY, CZ), F32),
            pltpu.SemaphoreType.DMA((8,)),
            pltpu.SemaphoreType.DMA((copies,)),
            pltpu.SemaphoreType.DMA((copies,)),
            pltpu.SemaphoreType.DMA((4,)),
            pltpu.SemaphoreType.REGULAR,
        ],
        compiler_params=pltpu.CompilerParams(
            collective_id=0, has_side_effects=True, vmem_limit_bytes=60 * 1024 * 1024
        ),
    )(
        temps, cotangent, solid_mask, patch_ids,
        heat_coeff.reshape(64, CZ), owner_slot.reshape(64, CZ),
    )
    return sens, patch


def solution(mesh):
    placed = (
        P(None, "gx", "gy", "gz"),
        P("gx", "gy", "gz"),
        P("gx", "gy", "gz"),
        P("gx", "gy", "gz"),
        P(),
        P(),
    )
    return jax.shard_map(
        on_device,
        mesh=mesh,
        in_specs=placed,
        out_specs=(P("gx", "gy", "gz"), P(("gx", "gy", "gz"))),
        check_vma=False,
    )
```

```python
import jax
import jax.numpy as jnp
from jax import lax
from jax.experimental import pallas as pl
from jax.experimental.pallas import tpu as pltpu
from jax.sharding import PartitionSpec as P

STEPS = 3
PATCH_PER = 16
GX, GY, GZ = 16, 16, 2
CX, CY, CZ = 32, 16, 128
Y0 = 8
F32 = jnp.float32
MESH = pl.DeviceIdType.MESH

time_step = 0.12
ambient = 0.6


def x_loop(unroll, body, init):
    def block(i, carry):
        stores = []
        for k in range(unroll):
            carry = body(i * unroll + k, carry, lambda *store: stores.append(store))
        for ref, index, value in stores:
            ref[index] = value
        return carry

    return lax.fori_loop(0, CX // unroll, block, init)


MASK, LAM, TEMP, PART, HEAT = range(5)


def kernel(
    temps, cot, mask, ids, heat, owner,
    sens, patch,
    comb, tpad, l2, lpad, mraw, idv, heatv, ownv, hv, mm, pe, tot,
    ysend, yrecv, corner, ycor, l2y, xcor,
    zsend, zrecv, zx, zy, zwork, accr, marks, arow, plane, rrow, zbuf,
    lsem, ssem, rsem, gsem, zsem,
):
    gx, gy, gz = lax.axis_index("gx"), lax.axis_index("gy"), lax.axis_index("gz")

    def in_plane(dx, dy, dc):
        x, y = lax.rem(gx // 4 + dx, 4), lax.rem(lax.rem(gx // 2, 2) * 2 + gz + dy, 4)
        return (x * 4 + y // 2 * 2 + lax.rem(gx + dc, 2), gy, lax.rem(y, 2))

    hops = lambda n, size: min(n, size - n)
    plane_peers = [(dx, dy, dc) for dx in range(4) for dy in range(4) for dc in range(2)][1:]
    plane_peers.sort(key=lambda d: -hops(d[0], 4) - hops(d[1], 4))
    column_peers = sorted(range(1, GY), key=lambda r: -hops(r, GY))

    def at(dx, dy, dz):
        return (lax.rem(gx + dx + GX, GX), lax.rem(gy + dy + GY, GY), 1 - gz if dz else gz)

    def in_column(r):
        return at(0, r, 0)

    barrier = pltpu.get_barrier_semaphore()
    near = [at(dx, dy, 0) for dx in (1, -1) for dy in (1, -1)]
    near += [in_plane(*d) for d in plane_peers[:10]]
    near += [in_column(r) for r in (4, -4, 3, -3, 2, -2, 1, -1)]
    near += [at(0, dy, 1) for dy in (1, -1)]
    near += [in_plane(*d) for d in plane_peers[10:]]
    for device in near:
        pl.semaphore_signal(barrier, inc=1, device_id=device, device_id_type=MESH)

    inner = (pl.ds(1, CX), pl.ds(Y0, CY))
    loads = [
        (mask, mraw), (cot, comb.at[LAM, pl.ds(1, CX)]), (temps.at[2], comb.at[TEMP, pl.ds(1, CX)]),
        (ids, idv), (heat, heatv), (owner, ownv),
        (temps.at[1], tpad.at[1].at[inner]),
        (temps.at[0], tpad.at[0].at[inner]),
    ]
    loads = [pltpu.make_async_copy(s, d, lsem.at[i]) for i, (s, d) in enumerate(loads)]
    for c in loads:
        c.start()
    for c in loads:
        c.wait()

    lane = lax.broadcasted_iota(jnp.int32, (CY, CZ), 1)
    row = lax.broadcasted_iota(jnp.int32, (CY, CZ), 0)
    lane8 = lax.broadcasted_iota(jnp.int32, (8, CZ), 1)
    lane32 = lax.broadcasted_iota(jnp.int32, (CX, CZ), 1)
    row32 = lax.broadcasted_iota(jnp.int32, (CX, CZ), 0)
    edge = jnp.where(gz == 0, CZ - 1, 0)
    ins = pl.ds(Y0, CY)

    def to_lane(value, target):
        return pltpu.roll(value, lax.rem(target - edge + CZ, CZ), 1)

    def from_lane(packed, source):
        return pltpu.roll(packed, lax.rem(edge - source + CZ, CZ), 1)

    def contribution(one, other):
        m, l, t, hl = one
        mo, lo, to = other
        g = 1.0 + 0.75 * (t * t) + to * (0.25 * to - 0.5 * t)
        return time_step * (m * mo) * (g * (lo - l) + hl)

    mraw_f = lambda x: mraw[x].astype(F32)

    def convert(x, carry, put):
        put(comb, (MASK, x + 1), mraw_f(x))
        return carry

    x_loop(8, convert, 0)
    zero = jnp.zeros((CY, CZ), F32)
    inside = lambda cond: jnp.where(cond, 1.0, 0.0).astype(F32)
    own_up_y, own_down_y = inside(row < CY - 1), inside(row > 0)
    own_up_z, own_down_z = inside(lane < CZ - 1), inside(lane > 0)

    def around(value):
        return (
            pltpu.roll(value, CY - 1, 0), pltpu.roll(value, 1, 0),
            pltpu.roll(value, CZ - 1, 1), pltpu.roll(value, 1, 1),
        )

    def before(x, carry, put):
        first, second = carry
        a = lax.rem(gx + x // (CX // 2), GX)
        picked = []
        for half in range(2):
            b = lax.rem(gy + half, GY)
            table = jnp.broadcast_to(heatv[pl.ds(a * 4 + b // 4, 1), :], (8, CZ))
            index = jnp.bitwise_and(idv[x, half * 8 : half * 8 + 8, :], CZ - 1)
            picked.append(jnp.take_along_axis(table, index, axis=1))
        h = jnp.concatenate(picked, axis=0)
        put(hv, x, h)
        m, l, t = comb[MASK, x + 1], comb[LAM, x + 1], comb[TEMP, x + 1]
        hl = h * l
        above, below = jnp.minimum(x + 2, CX), jnp.maximum(x, 1)
        ms = (comb[MASK, above] * inside(x < CX - 1), comb[MASK, below] * inside(x > 0))
        my = around(m)
        ms += (my[0] * own_up_y, my[1] * own_down_y, my[2] * own_up_z, my[3] * own_down_z)
        ls = (comb[LAM, above], comb[LAM, below]) + around(l)
        ts = (comb[TEMP, above], comb[TEMP, below]) + around(t)
        base, half_t = 1.0 + 0.75 * (t * t), 0.5 * t
        added = -6.0 * hl
        for mo, lo, to in zip(ms, ls, ts):
            added = added + mo * ((base + to * (0.25 * to - half_t)) * (lo - l) + hl)
        part = l + (time_step * m) * added
        put(comb, (PART, x + 1), part)
        put(comb, (HEAT, x + 1), hl)
        put(tot, x, (t - ambient) * l)
        for f, value in enumerate((m, l, t, part, hl)):
            put(ysend, (0, f, pl.ds(x, 1), slice(None)), value[:1])
            put(ysend, (1, f, pl.ds(x, 1), slice(None)), value[CY - 1 :])
        for f, value in enumerate((m, l, t, part)):
            first = jnp.where(lane == x + 32 * f, to_lane(value, x + 32 * f), first)
        for f, value in enumerate((hl, tpad[1, x + 1, ins, :], tpad[0, x + 1, ins, :])):
            second = jnp.where(lane == x + 32 * f, to_lane(value, x + 32 * f), second)
        return first, second

    first, second = x_loop(4, before, (zero, zero))
    zsend[0] = first
    zsend[1] = second

    b0, b1 = gy, lax.rem(gy + 1, GY)
    low8 = lax.rem(lane8 // 32, 2) == 0
    s16 = jnp.zeros((GX, CZ), jnp.int32)
    for yh, b in enumerate((b0, b1)):
        those = ownv[pl.ds(b // 4, GX, stride=4), :]
        for c in range(2):
            shift = lax.rem(2 * CZ + 48 * c + 16 * yh - 32 * lax.rem(b, 4), CZ)
            here_it_is = (lane // 64 == c) & (lax.rem(lane // 16, 2) == yh)
            s16 = jnp.where(here_it_is, pltpu.roll(those, shift, 1), s16)
    slots = jnp.where(low8, s16[:8], pltpu.roll(s16[8:], 32, 1))

    pl.semaphore_wait(barrier, len(near))

    counter = [0]

    def remote(src, dst, device):
        i = counter[0]
        counter[0] += 1
        copy = pltpu.make_async_remote_copy(
            src_ref=src, dst_ref=dst, send_sem=ssem.at[i], recv_sem=rsem.at[i],
            device_id=device, device_id_type=MESH,
        )
        copy.start()
        return copy

    def x_faces(ref):
        return [
            remote(ref.at[CX, ins], ref.at[0, ins], at(1, 0, 0)),
            remote(ref.at[1, ins], ref.at[CX + 1, ins], at(-1, 0, 0)),
        ]

    def y_faces(ref):
        xs = pl.ds(1, CX)
        return [
            remote(ref.at[xs, pl.ds(Y0 + CY - 1, 1)], ref.at[xs, pl.ds(Y0 - 1, 1)], at(0, 1, 0)),
            remote(ref.at[xs, pl.ds(Y0, 1)], ref.at[xs, pl.ds(Y0 + CY, 1)], at(0, -1, 0)),
        ]

    sent = []

    def landed(copies):
        sent.extend(copies)
        for c in copies:
            c.wait_recv()

    three = pl.ds(0, 3)
    round_1 = []
    for s, dx in ((0, 1), (1, -1)):
        for t, dy in ((0, 1), (1, -1)):
            x, y = (CX - 1 if dx == 1 else 0), (1 if dy == 1 else 0)
            round_1.append(remote(
                ysend.at[y, three, pl.ds(x, 1)], corner.at[s, t, three, pl.ds(0, 1)], at(dx, dy, 0)
            ))
    round_1 += [
        remote(comb.at[:, CX], comb.at[:, 0], at(1, 0, 0)),
        remote(comb.at[:, 1], comb.at[:, CX + 1], at(-1, 0, 0)),
        remote(zsend.at[0], zx.at[0], at(1, 0, 1)),
        remote(zsend.at[0], zx.at[1], at(-1, 0, 1)),
        remote(zsend.at[0], zy.at[0], at(0, 1, 1)),
        remote(zsend.at[0], zy.at[1], at(0, -1, 1)),
        remote(zsend.at[pl.ds(0, 2)], zrecv.at[pl.ds(0, 2)], at(0, 0, 1)),
        remote(ysend.at[1], yrecv.at[0], at(0, 1, 0)),
        remote(ysend.at[0], yrecv.at[1], at(0, -1, 0)),
    ]
    later_1 = [x_faces(tpad.at[i]) + y_faces(tpad.at[i]) for i in (1, 0)]
    for r in (4, -4):
        pl.semaphore_signal(zsem, inc=1, device_id=in_column(r), device_id_type=MESH)

    place = lax.rem(slots, PATCH_PER)
    which = lax.broadcasted_iota(jnp.int32, (CZ, CZ), 0)
    for r in range(8):
        hit = jnp.where(place[r : r + 1] == which, 1.0, 0.0)
        marks[r * CZ : (r + 1) * CZ, :] = jnp.transpose(hit).astype(jnp.bfloat16)
    landed(round_1)

    keep_x = (inside(gx > 0), inside(gx < GX - 1))
    keep_y = (inside(gy > 0), inside(gy < GY - 1))
    first_row, last_row = row == 0, row == CY - 1
    at_edge = inside(lane == edge)

    for s in range(2):
        mine, outer = (1, 0) if s == 0 else (CX, CX + 1)
        o = [comb[f, mine] for f in (MASK, LAM, TEMP, HEAT)]
        v = [comb[f, outer] for f in (MASK, LAM, TEMP, HEAT)]
        v[0] = v[0] * keep_x[s]
        xcor[s] = contribution(o, v[:3])
        new = comb[PART, outer] + contribution(v, o[:3])
        w = [jnp.where(first_row, corner[s, 0, f, :1, :], corner[s, 1, f, :1, :]) for f in range(3)]
        w[0] = w[0] * jnp.where(first_row, keep_y[0], jnp.where(last_row, keep_y[1], 0.0))
        new = new + contribution(v, w)
        source = CX - 1 if s == 0 else 0
        w = [from_lane(zx[s], 32 * f + source) for f in range(3)]
        w[0] = w[0] * at_edge
        l2[outer] = new + contribution(v, w)

    first_x, last_x = row32 == 0, row32 == CX - 1
    at_edge32 = inside(lane32 == edge)
    for t in range(2):
        o = [ysend[t, f] for f in (MASK, LAM, TEMP, HEAT)]
        v = [yrecv[t, f] for f in (MASK, LAM, TEMP, HEAT)]
        v[0] = v[0] * keep_y[t]
        ycor[t] = contribution(o, v[:3])
        new = yrecv[t, PART] + contribution(v, o[:3])
        w = [jnp.where(first_x, corner[0, t, f, :1, :], corner[1, t, f, :1, :]) for f in range(3)]
        w[0] = w[0] * jnp.where(first_x, keep_x[0], jnp.where(last_x, keep_x[1], 0.0))
        new = new + contribution(v, w)
        line = jnp.broadcast_to(zy[t, CY - 1 :, :] if t == 0 else zy[t, :1, :], (CX, CZ))
        w = [
            jnp.sum(jnp.where(lane32 == row32 + 32 * f, line, 0.0), axis=1, keepdims=True)
            for f in range(3)
        ]
        w = [jnp.broadcast_to(c, (CX, CZ)) for c in w]
        w[0] = w[0] * at_edge32
        l2y[t] = new + contribution(v, w)

    def group(packed, f):
        return packed if f == 0 else pltpu.roll(packed, CZ - 32 * f, 1)

    def moved(packed, source, target):
        shift = (target - source) % CZ
        return packed if shift == 0 else pltpu.roll(packed, shift, 1)

    o = [group(zsend[0], f) for f in range(3)] + [zsend[1]]
    v = [group(zrecv[0], f) for f in range(3)] + [zrecv[1]]
    zwork[0] = contribution(o, v[:3])
    new = group(zrecv[0], 3) + contribution(v, o[:3])
    w = [
        jnp.where(lane == 0, moved(zx[0], 32 * f + CX - 1, 0), moved(zx[1], 32 * f, CX - 1))
        for f in range(3)
    ]
    w[0] = w[0] * jnp.where(lane == 0, keep_x[0], jnp.where(lane == CX - 1, keep_x[1], 0.0))
    new = new + contribution(v, w)
    w = [
        jnp.where(first_row, group(zy[0, CY - 1 :, :], f), group(zy[1, :1, :], f))
        for f in range(3)
    ]
    w[0] = w[0] * jnp.where(first_row, keep_y[0], jnp.where(last_row, keep_y[1], 0.0))
    zwork[1] = new + contribution(v, w)

    def finish_1(x, carry, put):
        new = comb[PART, x + 1] + from_lane(zwork[0], x) * at_edge
        new = new + jnp.where(first_row, ycor[0, pl.ds(x, 1), :], 0.0)
        put(l2, x + 1, new + jnp.where(last_row, ycor[1, pl.ds(x, 1), :], 0.0))
        return carry

    x_loop(16, finish_1, 0)
    l2[1] = l2[1] + xcor[0]
    l2[CX] = l2[CX] + xcor[1]

    def z_neighbours(value, halo):
        up = jnp.where(lane == CZ - 1, halo, pltpu.roll(value, CZ - 1, 1))
        down = jnp.where(lane == 0, halo, pltpu.roll(value, 1, 1))
        return [up, down]

    def y_neighbours(value, up, down):
        return [
            jnp.where(last_row, up, pltpu.roll(value, CY - 1, 0)),
            jnp.where(first_row, down, pltpu.roll(value, 1, 0)),
        ]

    def six(ref, x, halo):
        here = ref[x + 1, ins, :]
        return here, [
            ref[x + 2, ins, :], ref[x, ins, :],
            ref[x + 1, pl.ds(Y0 + 1, CY), :], ref[x + 1, pl.ds(Y0 - 1, CY), :],
        ] + z_neighbours(here, halo)

    def masks(x, put):
        centre = comb[MASK, x + 1]
        up, down = z_neighbours(centre, from_lane(zrecv[0], x))
        others = [
            comb[MASK, x + 2] * inside((x < CX - 1) | (gx < GX - 1)),
            comb[MASK, x] * inside((x > 0) | (gx > 0)),
        ]
        others += y_neighbours(
            centre, yrecv[1, MASK, pl.ds(x, 1), :] * keep_y[1], yrecv[0, MASK, pl.ds(x, 1), :] * keep_y[0]
        )
        others += [
            up * jnp.where(lane == CZ - 1, inside(gz == 0), 1.0),
            down * jnp.where(lane == 0, inside(gz == 1), 1.0),
        ]
        active = others[0]
        for m in others[1:]:
            active = active + m
        scaled = time_step * centre
        surface = scaled * (6.0 - active)
        put(pe, x, surface)
        faces = [scaled * m for m in others]
        for d in range(6):
            put(mm, (d, x), faces[d])
        return faces, surface

    def coefficients(level, x, halo, faces, surface):
        here, there = six(tpad.at[level], x, halo)
        base = 1.0 + 0.75 * (here * here)
        half = 0.5 * here
        centre = 1.0 - surface * hv[x]
        out = []
        for t, m in zip(there, faces):
            k = m * (base + t * (0.25 * t - half))
            centre = centre - k
            out.append(k)
        return out, centre, here

    def apply(here, there, out, centre):
        new = centre * here
        for k, l in zip(out, there):
            new = new + k * l
        return new

    landed(later_1[0])

    def step_2(x, packed, put):
        faces, surface = masks(x, put)
        out, centre, t1 = coefficients(1, x, from_lane(zrecv[1], x + 32), faces, surface)
        here = l2[x + 1]
        there = [l2[x + 2], l2[x]]
        there += y_neighbours(here, l2y[1, pl.ds(x, 1), :], l2y[0, pl.ds(x, 1), :])
        there += z_neighbours(here, from_lane(zwork[1], x))
        new = apply(here, there, out, centre)
        put(lpad, (x + 1, ins, slice(None)), new)
        t0 = tpad[0, x + 1, ins, :]
        put(tot, x, -surface * (tot[x] + (t1 - ambient) * here + (t0 - ambient) * new))
        return jnp.where(lane == x, to_lane(new, x), packed)

    zsend[2] = x_loop(8, step_2, zero)

    for xh in range(2):
        def gather(i, accs):
            for k in range(4):
                x = xh * (CX // 2) + 4 * i + k
                value = tot[x]
                offset = jnp.bitwise_and(idv[x], PATCH_PER - 1)
                accs = [acc + jnp.where(offset == o, value, 0.0) for o, acc in enumerate(accs)]
            return accs

        accs = lax.fori_loop(0, CX // 8, gather, [zero] * PATCH_PER)
        for yh in range(2):
            for o in range(PATCH_PER):
                accr[pl.ds(((xh * 2 + yh) * PATCH_PER + o) * 8, 8), :] = accs[o][yh * 8 : yh * 8 + 8]
    folded = [accr[pl.ds(i, 4 * PATCH_PER, stride=8), :] for i in range(8)]
    while len(folded) > 1:
        folded = [a + b for a, b in zip(folded[::2], folded[1::2])]
    turned = jnp.transpose(folded[0])
    halves = []
    for half in range(2):
        parts = [turned[half * 64 + i * 8 : half * 64 + i * 8 + 8] for i in range(8)]
        while len(parts) > 1:
            parts = [a + b for a, b in zip(parts[::2], parts[1::2])]
        halves.append(parts[0])
    by_cell = [jnp.where(gz == c, halves[0], halves[1]) for c in range(2)]
    message = jnp.concatenate([jnp.sum(v, axis=0, keepdims=True) for v in by_cell], axis=1)
    arow[0:1, :] = message

    own_row = gz * GX + gx
    for d in plane_peers:
        pltpu.make_async_remote_copy(
            src_ref=arow.at[pl.ds(0, 1)], dst_ref=plane.at[pl.ds(own_row, 1)],
            send_sem=gsem.at[0], recv_sem=gsem.at[1],
            device_id=in_plane(*d), device_id_type=MESH,
        ).start()
    round_3 = x_faces(lpad) + y_faces(lpad) + [remote(zsend.at[2], zrecv.at[2], at(0, 0, 1))]
    landed(later_1[1])
    prepare_0 = lambda x: coefficients(
        0, x, from_lane(zrecv[1], x + 64), [mm[d, x] for d in range(6)], pe[x]
    )

    count = pl.ds(0, GX * GZ - 1)
    pltpu.make_async_copy(plane.at[count], plane.at[count], gsem.at[1]).wait()
    sums = jnp.where(row32 == own_row, message, plane[...])
    sums = sums[:GX] + sums[GX:]
    shifted = pltpu.roll(sums, CZ - 32, 1)
    sums = sums + jnp.concatenate([shifted[GX - 1 :], shifted[: GX - 1]], axis=0)
    sums = jnp.where(low8, sums[:8], pltpu.roll(sums[8:], 32, 1))

    mine = jnp.where((slots // 512 == gx) & (lax.rem(slots // 16, 2) == gz), sums, 0.0)
    target = lax.rem(slots // 32, GY)
    values = [jnp.where(target[r : r + 1] == row, mine[r : r + 1], 0.0) for r in range(8)]
    rest = jnp.concatenate(values, axis=1)
    pieces = []
    for _ in range(3):
        pieces.append(rest.astype(jnp.bfloat16))
        rest = rest - pieces[-1].astype(F32)
    share = lax.dot_general(
        jnp.concatenate(pieces, axis=0), marks[...], (((1,), (0,)), ((), ())),
        preferred_element_type=F32,
    )
    share = share[:GY] + share[GY : 2 * GY] + share[2 * GY :]
    rrow[...] = share
    pl.semaphore_wait(zsem, 2)
    for r in column_peers:
        to = in_column(r)
        pltpu.make_async_remote_copy(
            src_ref=rrow.at[pl.ds(to[1], 1)], dst_ref=zbuf.at[pl.ds(gy, 1)],
            send_sem=gsem.at[2], recv_sem=gsem.at[3],
            device_id=to, device_id_type=MESH,
        ).start()

    landed(round_3)

    def step_3(x, carry, put):
        out, centre, _ = prepare_0(x)
        here, there = six(lpad, x, from_lane(zrecv[2], x))
        put(sens, x, apply(here, there, out, centre))
        return carry

    x_loop(4, step_3, 0)
    for c in sent:
        c.wait_send()
    pltpu.make_async_copy(plane.at[count], plane.at[count], gsem.at[0]).wait()
    count = pl.ds(0, GY - 1)
    pltpu.make_async_copy(zbuf.at[count], zbuf.at[count], gsem.at[3]).wait()
    final = jnp.where(row == gy, share, zbuf[...])
    patch[...] = jnp.sum(final, axis=0)[:PATCH_PER]
    pltpu.make_async_copy(zbuf.at[count], zbuf.at[count], gsem.at[2]).wait()


def on_device(temps, cotangent, solid_mask, patch_ids, heat_coeff, owner_slot):
    anywhere = pl.BlockSpec(memory_space=pltpu.HBM)
    vmem = pl.BlockSpec(memory_space=pltpu.VMEM)
    field = (CX, CY, CZ)
    copies = 13 + 4 * 2 + 5
    sens, patch = pl.pallas_call(
        kernel,
        name="adjoint",
        out_shape=(
            pltpu.VMEM(field, F32),
            pltpu.VMEM((PATCH_PER,), F32),
        ),
        in_specs=[anywhere] * 6,
        out_specs=(vmem, vmem),
        scratch_shapes=[
            pltpu.VMEM((5, CX + 2, CY, CZ), F32),
            pltpu.VMEM((2, CX + 2, CY + 16, CZ), F32),
            pltpu.VMEM((CX + 2, CY, CZ), F32),
            pltpu.VMEM((CX + 2, CY + 16, CZ), F32),
            pltpu.VMEM(field, jnp.int32),
            pltpu.VMEM(field, jnp.int32),
            pltpu.VMEM((64, CZ), F32),
            pltpu.VMEM((64, CZ), jnp.int32),
            pltpu.VMEM(field, F32),
            pltpu.VMEM((6,) + field, F32),
            pltpu.VMEM(field, F32),
            pltpu.VMEM(field, F32),
            pltpu.VMEM((2, 5, CX, CZ), F32),
            pltpu.VMEM((2, 5, CX, CZ), F32),
            pltpu.VMEM((2, 2, 3, 8, CZ), F32),
            pltpu.VMEM((2, CX, CZ), F32),
            pltpu.VMEM((2, CX, CZ), F32),
            pltpu.VMEM((2, CY, CZ), F32),
            pltpu.VMEM((3, CY, CZ), F32),
            pltpu.VMEM((3, CY, CZ), F32),
            pltpu.VMEM((2, CY, CZ), F32),
            pltpu.VMEM((2, CY, CZ), F32),
            pltpu.VMEM((2, CY, CZ), F32),
            pltpu.VMEM((64 * 8, CZ), F32),
            pltpu.VMEM((8 * CZ, CZ), jnp.bfloat16),
            pltpu.VMEM((8, CZ), F32),
            pltpu.VMEM((GX * GZ, CZ), F32),
            pltpu.VMEM((GY, CZ), F32),
            pltpu.VMEM((GY, CZ), F32),
            pltpu.SemaphoreType.DMA((8,)),
            pltpu.SemaphoreType.DMA((copies,)),
            pltpu.SemaphoreType.DMA((copies,)),
            pltpu.SemaphoreType.DMA((4,)),
            pltpu.SemaphoreType.REGULAR,
        ],
        compiler_params=pltpu.CompilerParams(
            collective_id=0, has_side_effects=True, vmem_limit_bytes=60 * 1024 * 1024
        ),
    )(
        temps, cotangent, solid_mask, patch_ids,
        heat_coeff.reshape(64, CZ), owner_slot.reshape(64, CZ),
    )
    return sens, patch


def solution(mesh):
    placed = (
        P(None, "gx", "gy", "gz"),
        P("gx", "gy", "gz"),
        P("gx", "gy", "gz"),
        P("gx", "gy", "gz"),
        P(),
        P(),
    )
    return jax.shard_map(
        on_device,
        mesh=mesh,
        in_specs=placed,
        out_specs=(P("gx", "gy", "gz"), P(("gx", "gy", "gz"))),
        check_vma=False,
    )
```

```python
import jax
import jax.numpy as jnp
from jax import lax
from jax.experimental import pallas as pl
from jax.experimental.pallas import tpu as pltpu
from jax.sharding import PartitionSpec as P

STEPS = 3
PATCH_PER = 16
GX, GY, GZ = 16, 16, 2
CX, CY, CZ = 32, 16, 128
Y0 = 8
F32 = jnp.float32
MESH = pl.DeviceIdType.MESH

time_step = 0.12
ambient = 0.6


def x_loop(unroll, body, init):
    def block(i, carry):
        stores = []
        for k in range(unroll):
            ends = (k == 0, k == unroll - 1)
            carry = body(i * unroll + k, carry, lambda *store: stores.append(store), ends)
        for ref, index, value in stores:
            ref[index] = value
        return carry

    return lax.fori_loop(0, CX // unroll, block, init)


MASK, LAM, TEMP, PART, HEAT = range(5)
NEXT, COEFF = 5, 6


def kernel(
    temps, cot, mask, ids, heat, owner,
    sens, patch,
    comb, tpad, l2, lpad, mraw, idv, heatv, ownv, hv, kk, pe, tot,
    ysend, yrecv, corner, ycor, ype, yl2, l2y, xcor, xpe,
    zsend, zrecv, zx, zy, zwork, accr, marks, arow, plane, rrow, zbuf,
    lsem, ssem, rsem, gsem, zsem,
):
    gx, gy, gz = lax.axis_index("gx"), lax.axis_index("gy"), lax.axis_index("gz")

    def in_plane(dx, dy, dc):
        x, y = lax.rem(gx // 4 + dx, 4), lax.rem(lax.rem(gx // 2, 2) * 2 + gz + dy, 4)
        return (x * 4 + y // 2 * 2 + lax.rem(gx + dc, 2), gy, lax.rem(y, 2))

    hops = lambda n, size: min(n, size - n)
    plane_peers = [(dx, dy, dc) for dx in range(4) for dy in range(4) for dc in range(2)][1:]
    plane_peers.sort(key=lambda d: -hops(d[0], 4) - hops(d[1], 4))
    column_peers = sorted(range(1, GY), key=lambda r: -hops(r, GY))

    def at(dx, dy, dz):
        return (lax.rem(gx + dx + GX, GX), lax.rem(gy + dy + GY, GY), 1 - gz if dz else gz)

    def in_column(r):
        return at(0, r, 0)

    barrier = pltpu.get_barrier_semaphore()
    near = [at(dx, dy, 0) for dx in (1, -1) for dy in (1, -1)]
    near += [in_plane(*d) for d in plane_peers[:10]]
    near += [in_column(r) for r in (4, -4, 3, -3, 2, -2, 1, -1)]
    near += [at(0, dy, 1) for dy in (1, -1)]
    near += [in_plane(*d) for d in plane_peers[10:]]
    for device in near:
        pl.semaphore_signal(barrier, inc=1, device_id=device, device_id_type=MESH)

    inner = (pl.ds(1, CX), pl.ds(Y0, CY))
    loads = [
        (mask, mraw), (cot, comb.at[LAM, pl.ds(1, CX)]), (temps.at[2], comb.at[TEMP, pl.ds(1, CX)]),
        (ids, idv), (heat, heatv), (owner, ownv),
        (temps.at[1], tpad.at[1].at[inner]),
        (temps.at[0], tpad.at[0].at[inner]),
    ]
    loads = [pltpu.make_async_copy(s, d, lsem.at[i]) for i, (s, d) in enumerate(loads)]
    for c in loads:
        c.start()
    for c in loads:
        c.wait()

    lane = lax.broadcasted_iota(jnp.int32, (CY, CZ), 1)
    row = lax.broadcasted_iota(jnp.int32, (CY, CZ), 0)
    lane8 = lax.broadcasted_iota(jnp.int32, (8, CZ), 1)
    lane32 = lax.broadcasted_iota(jnp.int32, (CX, CZ), 1)
    row32 = lax.broadcasted_iota(jnp.int32, (CX, CZ), 0)
    edge = jnp.where(gz == 0, CZ - 1, 0)
    ins = pl.ds(Y0, CY)

    def to_lane(value, target):
        return pltpu.roll(value, lax.rem(target - edge + CZ, CZ), 1)

    def from_lane(packed, source):
        return pltpu.roll(packed, lax.rem(edge - source + CZ, CZ), 1)

    def contribution(one, other):
        m, l, t, hl = one
        mo, lo, to = other
        g = 1.0 + 0.75 * (t * t) + to * (0.25 * to - 0.5 * t)
        return time_step * (m * mo) * (g * (lo - l) + hl)

    mraw_f = lambda x: mraw[x].astype(F32)

    def convert(x, carry, put, ends):
        put(comb, (MASK, x + 1), mraw_f(x))
        return carry

    x_loop(8, convert, 0)
    zero = jnp.zeros((CY, CZ), F32)
    inside = lambda cond: jnp.where(cond, 1.0, 0.0).astype(F32)
    own_up_y, own_down_y = inside(row < CY - 1), inside(row > 0)
    own_up_z, own_down_z = inside(lane < CZ - 1), inside(lane > 0)

    def around(value):
        return (
            pltpu.roll(value, CY - 1, 0), pltpu.roll(value, 1, 0),
            pltpu.roll(value, CZ - 1, 1), pltpu.roll(value, 1, 1),
        )

    def before(x, carry, put, ends):
        first, second = carry
        a = lax.rem(gx + x // (CX // 2), GX)
        picked = []
        for half in range(2):
            b = lax.rem(gy + half, GY)
            table = jnp.broadcast_to(heatv[pl.ds(a * 4 + b // 4, 1), :], (8, CZ))
            index = jnp.bitwise_and(idv[x, half * 8 : half * 8 + 8, :], CZ - 1)
            picked.append(jnp.take_along_axis(table, index, axis=1))
        h = jnp.concatenate(picked, axis=0)
        put(hv, x, h)
        m, l, t = comb[MASK, x + 1], comb[LAM, x + 1], comb[TEMP, x + 1]
        hl = h * l
        above, below = jnp.minimum(x + 2, CX), jnp.maximum(x, 1)
        ms = (comb[MASK, above] * inside(x < CX - 1), comb[MASK, below] * inside(x > 0))
        my = around(m)
        ms += (my[0] * own_up_y, my[1] * own_down_y, my[2] * own_up_z, my[3] * own_down_z)
        ls = (comb[LAM, above], comb[LAM, below]) + around(l)
        ts = (comb[TEMP, above], comb[TEMP, below]) + around(t)
        base, half_t = 1.0 + 0.75 * (t * t), 0.5 * t
        added = -6.0 * hl
        for mo, lo, to in zip(ms, ls, ts):
            added = added + mo * ((base + to * (0.25 * to - half_t)) * (lo - l) + hl)
        part = l + (time_step * m) * added
        put(comb, (PART, x + 1), part)
        put(comb, (HEAT, x + 1), hl)
        put(tot, x, (t - ambient) * l)
        t1 = tpad[1, x + 1, ins, :]
        for f, value in enumerate((m, l, t, part, hl, t1, h)):
            put(ysend, (0, f, pl.ds(x, 1), slice(None)), value[:1])
            put(ysend, (1, f, pl.ds(x, 1), slice(None)), value[CY - 1 :])
        for f, value in enumerate((m, l, t, part)):
            first = jnp.where(lane == x + 32 * f, to_lane(value, x + 32 * f), first)
        for f, value in enumerate((hl, t1, tpad[0, x + 1, ins, :], h)):
            second = jnp.where(lane == x + 32 * f, to_lane(value, x + 32 * f), second)
        return first, second

    first, second = x_loop(4, before, (zero, zero))
    zsend[0] = first
    zsend[1] = second

    b0, b1 = gy, lax.rem(gy + 1, GY)
    low8 = lax.rem(lane8 // 32, 2) == 0
    s16 = jnp.zeros((GX, CZ), jnp.int32)
    for yh, b in enumerate((b0, b1)):
        those = ownv[pl.ds(b // 4, GX, stride=4), :]
        for c in range(2):
            shift = lax.rem(2 * CZ + 48 * c + 16 * yh - 32 * lax.rem(b, 4), CZ)
            here_it_is = (lane // 64 == c) & (lax.rem(lane // 16, 2) == yh)
            s16 = jnp.where(here_it_is, pltpu.roll(those, shift, 1), s16)
    slots = jnp.where(low8, s16[:8], pltpu.roll(s16[8:], 32, 1))

    pl.semaphore_wait(barrier, len(near))

    counter = [0]

    def remote(src, dst, device):
        i = counter[0]
        counter[0] += 1
        copy = pltpu.make_async_remote_copy(
            src_ref=src, dst_ref=dst, send_sem=ssem.at[i], recv_sem=rsem.at[i],
            device_id=device, device_id_type=MESH,
        )
        copy.start()
        return copy

    def x_faces(ref):
        return [
            remote(ref.at[CX, ins], ref.at[0, ins], at(1, 0, 0)),
            remote(ref.at[1, ins], ref.at[CX + 1, ins], at(-1, 0, 0)),
        ]

    def y_faces(ref):
        xs = pl.ds(1, CX)
        return [
            remote(ref.at[xs, pl.ds(Y0 + CY - 1, 1)], ref.at[xs, pl.ds(Y0 - 1, 1)], at(0, 1, 0)),
            remote(ref.at[xs, pl.ds(Y0, 1)], ref.at[xs, pl.ds(Y0 + CY, 1)], at(0, -1, 0)),
        ]

    sent = []

    def landed(copies):
        sent.extend(copies)
        for c in copies:
            c.wait_recv()

    three, five = pl.ds(0, 3), pl.ds(0, 5)
    round_1 = []
    for s, dx in ((0, 1), (1, -1)):
        for t, dy in ((0, 1), (1, -1)):
            x, y = (CX - 1 if dx == 1 else 0), (1 if dy == 1 else 0)
            round_1.append(remote(
                ysend.at[y, three, pl.ds(x, 1)], corner.at[s, t, three, pl.ds(0, 1)], at(dx, dy, 0)
            ))
    round_1 += [
        remote(comb.at[:, CX], comb.at[:, 0], at(1, 0, 0)),
        remote(comb.at[:, 1], comb.at[:, CX + 1], at(-1, 0, 0)),
        remote(zsend.at[0], zx.at[0], at(1, 0, 1)),
        remote(zsend.at[0], zx.at[1], at(-1, 0, 1)),
        remote(zsend.at[0], zy.at[0], at(0, 1, 1)),
        remote(zsend.at[0], zy.at[1], at(0, -1, 1)),
        remote(zsend.at[pl.ds(0, 2)], zrecv.at[pl.ds(0, 2)], at(0, 0, 1)),
        remote(ysend.at[1, five], yrecv.at[0, five], at(0, 1, 0)),
        remote(ysend.at[0, five], yrecv.at[1, five], at(0, -1, 0)),
    ]
    later_1 = [
        x_faces(tpad.at[1]) + [
            remote(ysend.at[1, NEXT], yrecv.at[0, NEXT], at(0, 1, 0)),
            remote(ysend.at[0, NEXT], yrecv.at[1, NEXT], at(0, -1, 0)),
        ],
        x_faces(tpad.at[0]) + y_faces(tpad.at[0]),
    ]
    for r in (4, -4):
        pl.semaphore_signal(zsem, inc=1, device_id=in_column(r), device_id_type=MESH)

    place = lax.rem(slots, PATCH_PER)
    which = lax.broadcasted_iota(jnp.int32, (CZ, CZ), 0)
    for r in range(8):
        hit = jnp.where(place[r : r + 1] == which, 1.0, 0.0)
        marks[r * CZ : (r + 1) * CZ, :] = jnp.transpose(hit).astype(jnp.bfloat16)

    def prepare_1(x, carry, put, ends):
        m, t, h = comb[MASK, x + 1], tpad[1, x + 1, ins, :], hv[x]
        above, below = jnp.minimum(x + 2, CX), jnp.maximum(x, 1)
        my = around(m)
        ms = (
            comb[MASK, above] * inside(x < CX - 1), comb[MASK, below] * inside(x > 0),
            my[0] * own_up_y, my[1] * own_down_y, my[2] * own_up_z, my[3] * own_down_z,
        )
        ts = (tpad[1, above, ins, :], tpad[1, below, ins, :]) + around(t)
        base, half_t = 1.0 + 0.75 * (t * t), 0.5 * t
        scaled, active = time_step * m, zero
        total = zero
        for d, (mo, to) in enumerate(zip(ms, ts)):
            k = (scaled * mo) * (base + to * (0.25 * to - half_t))
            active = active + mo
            total = total + k
            put(kk, (d, x), k)
        surface = scaled * (6.0 - active)
        put(kk, (6, x), 1.0 - surface * h - total)
        put(pe, x, surface)
        return carry

    x_loop(4, prepare_1, 0)
    landed(round_1)

    keep_x = (inside(gx > 0), inside(gx < GX - 1))
    keep_y = (inside(gy > 0), inside(gy < GY - 1))
    first_row, last_row = row == 0, row == CY - 1
    at_edge = inside(lane == edge)

    for s in range(2):
        mine, outer = (1, 0) if s == 0 else (CX, CX + 1)
        o = [comb[f, mine] for f in (MASK, LAM, TEMP, HEAT)]
        v = [comb[f, outer] for f in (MASK, LAM, TEMP, HEAT)]
        v[0] = v[0] * keep_x[s]
        xcor[s] = contribution(o, v[:3])
        new = comb[PART, outer] + contribution(v, o[:3])
        w = [jnp.where(first_row, corner[s, 0, f, :1, :], corner[s, 1, f, :1, :]) for f in range(3)]
        w[0] = w[0] * jnp.where(first_row, keep_y[0], jnp.where(last_row, keep_y[1], 0.0))
        new = new + contribution(v, w)
        source = CX - 1 if s == 0 else 0
        w = [from_lane(zx[s], 32 * f + source) for f in range(3)]
        w[0] = w[0] * at_edge
        l2[outer] = new + contribution(v, w)

    first_x, last_x = row32 == 0, row32 == CX - 1
    at_edge32 = inside(lane32 == edge)
    for t in range(2):
        o = [ysend[t, f] for f in (MASK, LAM, TEMP, HEAT)]
        v = [yrecv[t, f] for f in (MASK, LAM, TEMP, HEAT)]
        v[0] = v[0] * keep_y[t]
        ycor[t] = contribution(o, v[:3])
        new = yrecv[t, PART] + contribution(v, o[:3])
        w = [jnp.where(first_x, corner[0, t, f, :1, :], corner[1, t, f, :1, :]) for f in range(3)]
        w[0] = w[0] * jnp.where(first_x, keep_x[0], jnp.where(last_x, keep_x[1], 0.0))
        new = new + contribution(v, w)
        line = jnp.broadcast_to(zy[t, CY - 1 :, :] if t == 0 else zy[t, :1, :], (CX, CZ))
        w = [
            jnp.sum(jnp.where(lane32 == row32 + 32 * f, line, 0.0), axis=1, keepdims=True)
            for f in range(3)
        ]
        w = [jnp.broadcast_to(c, (CX, CZ)) for c in w]
        w[0] = w[0] * at_edge32
        l2y[t] = new + contribution(v, w)

    def group(packed, f):
        return packed if f == 0 else pltpu.roll(packed, CZ - 32 * f, 1)

    def moved(packed, source, target):
        shift = (target - source) % CZ
        return packed if shift == 0 else pltpu.roll(packed, shift, 1)

    o = [group(zsend[0], f) for f in range(3)] + [zsend[1]]
    v = [group(zrecv[0], f) for f in range(3)] + [zrecv[1]]
    zwork[0] = contribution(o, v[:3])
    new = group(zrecv[0], 3) + contribution(v, o[:3])
    w = [
        jnp.where(lane == 0, moved(zx[0], 32 * f + CX - 1, 0), moved(zx[1], 32 * f, CX - 1))
        for f in range(3)
    ]
    w[0] = w[0] * jnp.where(lane == 0, keep_x[0], jnp.where(lane == CX - 1, keep_x[1], 0.0))
    new = new + contribution(v, w)
    w = [
        jnp.where(first_row, group(zy[0, CY - 1 :, :], f), group(zy[1, :1, :], f))
        for f in range(3)
    ]
    w[0] = w[0] * jnp.where(first_row, keep_y[0], jnp.where(last_row, keep_y[1], 0.0))
    zwork[1] = new + contribution(v, w)

    def faces_of(x, refs, ends):
        xref, yref, zref = refs
        out = from_lane(zref[...], x) * at_edge
        out = out + jnp.where(
            first_row, yref[0, pl.ds(x, 1), :], jnp.where(last_row, yref[1, pl.ds(x, 1), :], 0.0)
        )
        if ends[0]:
            out = out + xref[0] * inside(x == 0)
        if ends[1]:
            out = out + xref[1] * inside(x == CX - 1)
        return out

    def finish_1(x, packed, put, ends):
        new = comb[PART, x + 1] + faces_of(x, (xcor, ycor, zwork.at[0]), ends)
        put(l2, x + 1, new)
        put(yl2, (0, pl.ds(x, 1), slice(None)), new[:1])
        put(yl2, (1, pl.ds(x, 1), slice(None)), new[CY - 1 :])
        return jnp.where(lane == x, to_lane(new, x), packed)

    zl2 = x_loop(16, finish_1, zero)
    landed(later_1[0])

    for s in range(2):
        mine, outer = (1, 0) if s == 0 else (CX, CX + 1)
        l = l2[mine]
        m, mo = comb[MASK, mine], comb[MASK, outer] * keep_x[s]
        xcor[s] = contribution(
            (m, l, tpad[1, mine, ins, :], hv[mine - 1] * l), (mo, l2[outer], tpad[1, outer, ins, :])
        )
        xpe[s] = -time_step * (m * mo)
    for t in range(2):
        l = yl2[t]
        m, mo = ysend[t, MASK], yrecv[t, MASK] * keep_y[t]
        ycor[t] = contribution(
            (m, l, ysend[t, NEXT], ysend[t, COEFF] * l), (mo, l2y[t], yrecv[t, NEXT])
        )
        ype[t] = -time_step * (m * mo)
    m, mo = zsend[0], zrecv[0]
    zwork[0] = contribution(
        (m, zl2, group(zsend[1], 1), group(zsend[1], 3) * zl2), (mo, zwork[1], group(zrecv[1], 1))
    )
    zwork[2] = -time_step * (m * mo)

    def z_neighbours(value, halo):
        up = jnp.where(lane == CZ - 1, halo, pltpu.roll(value, CZ - 1, 1))
        down = jnp.where(lane == 0, halo, pltpu.roll(value, 1, 1))
        return [up, down]

    def y_neighbours(value, up, down):
        return [
            jnp.where(last_row, up, pltpu.roll(value, CY - 1, 0)),
            jnp.where(first_row, down, pltpu.roll(value, 1, 0)),
        ]

    def six(ref, x, halo):
        here = ref[x + 1, ins, :]
        return here, [
            ref[x + 2, ins, :], ref[x, ins, :],
            ref[x + 1, pl.ds(Y0 + 1, CY), :], ref[x + 1, pl.ds(Y0 - 1, CY), :],
        ] + z_neighbours(here, halo)

    def masks(x):
        centre = comb[MASK, x + 1]
        up, down = z_neighbours(centre, from_lane(zrecv[0], x))
        others = [
            comb[MASK, x + 2] * inside((x < CX - 1) | (gx < GX - 1)),
            comb[MASK, x] * inside((x > 0) | (gx > 0)),
        ]
        others += y_neighbours(
            centre, yrecv[1, MASK, pl.ds(x, 1), :] * keep_y[1], yrecv[0, MASK, pl.ds(x, 1), :] * keep_y[0]
        )
        others += [
            up * jnp.where(lane == CZ - 1, inside(gz == 0), 1.0),
            down * jnp.where(lane == 0, inside(gz == 1), 1.0),
        ]
        active = others[0]
        for m in others[1:]:
            active = active + m
        scaled = time_step * centre
        surface = scaled * (6.0 - active)
        return [scaled * m for m in others], surface

    def coefficients(level, x, halo, faces, surface):
        here, there = six(tpad.at[level], x, halo)
        base = 1.0 + 0.75 * (here * here)
        half = 0.5 * here
        centre = 1.0 - surface * hv[x]
        out = []
        for t, m in zip(there, faces):
            k = m * (base + t * (0.25 * t - half))
            centre = centre - k
            out.append(k)
        return out, centre, here

    def apply(here, there, out, centre):
        new = centre * here
        for k, l in zip(out, there):
            new = new + k * l
        return new

    def step_2(x, packed, put, ends):
        here = l2[x + 1]
        there = (l2[x + 2], l2[x]) + around(here)
        new = apply(here, there, [kk[d, x] for d in range(6)], kk[6, x])
        new = new + faces_of(x, (xcor, ycor, zwork.at[0]), ends)
        surface = pe[x] + faces_of(x, (xpe, ype, zwork.at[2]), ends)
        put(lpad, (x + 1, ins, slice(None)), new)
        t0, t1 = tpad[0, x + 1, ins, :], tpad[1, x + 1, ins, :]
        put(tot, x, -surface * (tot[x] + (t1 - ambient) * here + (t0 - ambient) * new))
        return jnp.where(lane == x, to_lane(new, x), packed)

    zsend[2] = x_loop(16, step_2, zero)

    for xh in range(2):
        def gather(i, accs):
            for k in range(4):
                x = xh * (CX // 2) + 4 * i + k
                value = tot[x]
                offset = jnp.bitwise_and(idv[x], PATCH_PER - 1)
                accs = [acc + jnp.where(offset == o, value, 0.0) for o, acc in enumerate(accs)]
            return accs

        accs = lax.fori_loop(0, CX // 8, gather, [zero] * PATCH_PER)
        for yh in range(2):
            for o in range(PATCH_PER):
                accr[pl.ds(((xh * 2 + yh) * PATCH_PER + o) * 8, 8), :] = accs[o][yh * 8 : yh * 8 + 8]
    folded = [accr[pl.ds(i, 4 * PATCH_PER, stride=8), :] for i in range(8)]
    while len(folded) > 1:
        folded = [a + b for a, b in zip(folded[::2], folded[1::2])]
    turned = jnp.transpose(folded[0])
    halves = []
    for half in range(2):
        parts = [turned[half * 64 + i * 8 : half * 64 + i * 8 + 8] for i in range(8)]
        while len(parts) > 1:
            parts = [a + b for a, b in zip(parts[::2], parts[1::2])]
        halves.append(parts[0])
    by_cell = [jnp.where(gz == c, halves[0], halves[1]) for c in range(2)]
    message = jnp.concatenate([jnp.sum(v, axis=0, keepdims=True) for v in by_cell], axis=1)
    arow[0:1, :] = message

    own_row = gz * GX + gx
    for d in plane_peers:
        pltpu.make_async_remote_copy(
            src_ref=arow.at[pl.ds(0, 1)], dst_ref=plane.at[pl.ds(own_row, 1)],
            send_sem=gsem.at[0], recv_sem=gsem.at[1],
            device_id=in_plane(*d), device_id_type=MESH,
        ).start()
    round_3 = x_faces(lpad) + y_faces(lpad) + [remote(zsend.at[2], zrecv.at[2], at(0, 0, 1))]
    landed(later_1[1])

    count = pl.ds(0, GX * GZ - 1)
    pltpu.make_async_copy(plane.at[count], plane.at[count], gsem.at[1]).wait()
    sums = jnp.where(row32 == own_row, message, plane[...])
    sums = sums[:GX] + sums[GX:]
    shifted = pltpu.roll(sums, CZ - 32, 1)
    sums = sums + jnp.concatenate([shifted[GX - 1 :], shifted[: GX - 1]], axis=0)
    sums = jnp.where(low8, sums[:8], pltpu.roll(sums[8:], 32, 1))

    mine = jnp.where((slots // 512 == gx) & (lax.rem(slots // 16, 2) == gz), sums, 0.0)
    target = lax.rem(slots // 32, GY)
    values = [jnp.where(target[r : r + 1] == row, mine[r : r + 1], 0.0) for r in range(8)]
    rest = jnp.concatenate(values, axis=1)
    pieces = []
    for _ in range(3):
        pieces.append(rest.astype(jnp.bfloat16))
        rest = rest - pieces[-1].astype(F32)
    share = lax.dot_general(
        jnp.concatenate(pieces, axis=0), marks[...], (((1,), (0,)), ((), ())),
        preferred_element_type=F32,
    )
    share = share[:GY] + share[GY : 2 * GY] + share[2 * GY :]
    rrow[...] = share
    pl.semaphore_wait(zsem, 2)
    for r in column_peers:
        to = in_column(r)
        pltpu.make_async_remote_copy(
            src_ref=rrow.at[pl.ds(to[1], 1)], dst_ref=zbuf.at[pl.ds(gy, 1)],
            send_sem=gsem.at[2], recv_sem=gsem.at[3],
            device_id=to, device_id_type=MESH,
        ).start()

    landed(round_3)

    def step_3(x, carry, put, ends):
        out, centre, _ = coefficients(0, x, from_lane(zrecv[1], x + 64), *masks(x))
        here, there = six(lpad, x, from_lane(zrecv[2], x))
        put(sens, x, apply(here, there, out, centre))
        return carry

    x_loop(4, step_3, 0)
    for c in sent:
        c.wait_send()
    pltpu.make_async_copy(plane.at[count], plane.at[count], gsem.at[0]).wait()
    count = pl.ds(0, GY - 1)
    pltpu.make_async_copy(zbuf.at[count], zbuf.at[count], gsem.at[3]).wait()
    final = jnp.where(row == gy, share, zbuf[...])
    patch[...] = jnp.sum(final, axis=0)[:PATCH_PER]
    pltpu.make_async_copy(zbuf.at[count], zbuf.at[count], gsem.at[2]).wait()


def on_device(temps, cotangent, solid_mask, patch_ids, heat_coeff, owner_slot):
    anywhere = pl.BlockSpec(memory_space=pltpu.HBM)
    vmem = pl.BlockSpec(memory_space=pltpu.VMEM)
    field = (CX, CY, CZ)
    copies = 13 + 4 * 2 + 5
    sens, patch = pl.pallas_call(
        kernel,
        name="adjoint",
        out_shape=(
            pltpu.VMEM(field, F32),
            pltpu.VMEM((PATCH_PER,), F32),
        ),
        in_specs=[anywhere] * 6,
        out_specs=(vmem, vmem),
        scratch_shapes=[
            pltpu.VMEM((5, CX + 2, CY, CZ), F32),
            pltpu.VMEM((2, CX + 2, CY + 16, CZ), F32),
            pltpu.VMEM((CX + 2, CY, CZ), F32),
            pltpu.VMEM((CX + 2, CY + 16, CZ), F32),
            pltpu.VMEM(field, jnp.int32),
            pltpu.VMEM(field, jnp.int32),
            pltpu.VMEM((64, CZ), F32),
            pltpu.VMEM((64, CZ), jnp.int32),
            pltpu.VMEM(field, F32),
            pltpu.VMEM((7,) + field, F32),
            pltpu.VMEM(field, F32),
            pltpu.VMEM(field, F32),
            pltpu.VMEM((2, 7, CX, CZ), F32),
            pltpu.VMEM((2, 6, CX, CZ), F32),
            pltpu.VMEM((2, 2, 3, 8, CZ), F32),
            pltpu.VMEM((2, CX, CZ), F32),
            pltpu.VMEM((2, CX, CZ), F32),
            pltpu.VMEM((2, CX, CZ), F32),
            pltpu.VMEM((2, CX, CZ), F32),
            pltpu.VMEM((2, CY, CZ), F32),
            pltpu.VMEM((2, CY, CZ), F32),
            pltpu.VMEM((3, CY, CZ), F32),
            pltpu.VMEM((3, CY, CZ), F32),
            pltpu.VMEM((2, CY, CZ), F32),
            pltpu.VMEM((2, CY, CZ), F32),
            pltpu.VMEM((3, CY, CZ), F32),
            pltpu.VMEM((64 * 8, CZ), F32),
            pltpu.VMEM((8 * CZ, CZ), jnp.bfloat16),
            pltpu.VMEM((8, CZ), F32),
            pltpu.VMEM((GX * GZ, CZ), F32),
            pltpu.VMEM((GY, CZ), F32),
            pltpu.VMEM((GY, CZ), F32),
            pltpu.SemaphoreType.DMA((8,)),
            pltpu.SemaphoreType.DMA((copies,)),
            pltpu.SemaphoreType.DMA((copies,)),
            pltpu.SemaphoreType.DMA((4,)),
            pltpu.SemaphoreType.REGULAR,
        ],
        compiler_params=pltpu.CompilerParams(
            collective_id=0, has_side_effects=True, vmem_limit_bytes=60 * 1024 * 1024
        ),
    )(
        temps, cotangent, solid_mask, patch_ids,
        heat_coeff.reshape(64, CZ), owner_slot.reshape(64, CZ),
    )
    return sens, patch


def solution(mesh):
    placed = (
        P(None, "gx", "gy", "gz"),
        P("gx", "gy", "gz"),
        P("gx", "gy", "gz"),
        P("gx", "gy", "gz"),
        P(),
        P(),
    )
    return jax.shard_map(
        on_device,
        mesh=mesh,
        in_specs=placed,
        out_specs=(P("gx", "gy", "gz"), P(("gx", "gy", "gz"))),
        check_vma=False,
    )
```

```python
import jax
import jax.numpy as jnp
from jax import lax
from jax.experimental import pallas as pl
from jax.experimental.pallas import tpu as pltpu
from jax.sharding import PartitionSpec as P

STEPS = 3
PATCH_PER = 16
GX, GY, GZ = 16, 16, 2
CX, CY, CZ = 32, 16, 128
Y0 = 8
F32 = jnp.float32
MESH = pl.DeviceIdType.MESH

time_step = 0.12
ambient = 0.6


def x_loop(unroll, body, init):
    def block(i, carry):
        stores = []
        for k in range(unroll):
            ends = (k == 0, k == unroll - 1)
            carry = body(i * unroll + k, carry, lambda *store: stores.append(store), ends)
        for ref, index, value in stores:
            ref[index] = value
        return carry

    return lax.fori_loop(0, CX // unroll, block, init)


MASK, LAM, TEMP, PART, HEAT = range(5)
NEXT, COEFF = 5, 6


def kernel(
    temps, cot, mask, ids, heat, owner,
    sens, patch,
    comb, tpad, l2, lpad, mraw, idv, heatv, ownv, hv, kk, pe, tot,
    ysend, yrecv, corner, ycor, ype, yl2, l2y, xcor, xpe,
    zsend, zrecv, zx, zy, zwork, accr, marks, arow, plane, rrow, zbuf,
    lsem, ssem, rsem, gsem, zsem,
):
    gx, gy, gz = lax.axis_index("gx"), lax.axis_index("gy"), lax.axis_index("gz")

    def in_plane(dx, dy, dc):
        x, y = lax.rem(gx // 4 + dx, 4), lax.rem(lax.rem(gx // 2, 2) * 2 + gz + dy, 4)
        return (x * 4 + y // 2 * 2 + lax.rem(gx + dc, 2), gy, lax.rem(y, 2))

    hops = lambda n, size: min(n, size - n)
    plane_peers = [(dx, dy, dc) for dx in range(4) for dy in range(4) for dc in range(2)][1:]
    plane_peers.sort(key=lambda d: -hops(d[0], 4) - hops(d[1], 4))
    column_peers = sorted(range(1, GY), key=lambda r: -hops(r, GY))

    def at(dx, dy, dz):
        return (lax.rem(gx + dx + GX, GX), lax.rem(gy + dy + GY, GY), 1 - gz if dz else gz)

    def in_column(r):
        return at(0, r, 0)

    barrier = pltpu.get_barrier_semaphore()
    near = [at(dx, dy, 0) for dx in (1, -1) for dy in (1, -1)]
    near += [in_plane(*d) for d in plane_peers[:10]]
    near += [in_column(r) for r in (4, -4, 3, -3, 2, -2, 1, -1)]
    near += [at(0, dy, 1) for dy in (1, -1)]
    near += [in_plane(*d) for d in plane_peers[10:]]
    for device in near:
        pl.semaphore_signal(barrier, inc=1, device_id=device, device_id_type=MESH)

    inner = (pl.ds(1, CX), pl.ds(Y0, CY))
    loads = [
        (mask, mraw), (cot, comb.at[LAM, pl.ds(1, CX)]), (temps.at[2], comb.at[TEMP, pl.ds(1, CX)]),
        (ids, idv), (heat, heatv), (owner, ownv),
        (temps.at[1], tpad.at[1].at[inner]),
        (temps.at[0], tpad.at[0].at[inner]),
    ]
    loads = [pltpu.make_async_copy(s, d, lsem.at[i]) for i, (s, d) in enumerate(loads)]
    for c in loads:
        c.start()
    for c in loads:
        c.wait()

    lane = lax.broadcasted_iota(jnp.int32, (CY, CZ), 1)
    row = lax.broadcasted_iota(jnp.int32, (CY, CZ), 0)
    lane8 = lax.broadcasted_iota(jnp.int32, (8, CZ), 1)
    lane32 = lax.broadcasted_iota(jnp.int32, (CX, CZ), 1)
    row32 = lax.broadcasted_iota(jnp.int32, (CX, CZ), 0)
    edge = jnp.where(gz == 0, CZ - 1, 0)
    ins = pl.ds(Y0, CY)

    def to_lane(value, target):
        return pltpu.roll(value, lax.rem(target - edge + CZ, CZ), 1)

    def from_lane(packed, source):
        return pltpu.roll(packed, lax.rem(edge - source + CZ, CZ), 1)

    def contribution(one, other):
        m, l, t, hl = one
        mo, lo, to = other
        g = 1.0 + 0.75 * (t * t) + to * (0.25 * to - 0.5 * t)
        return time_step * (m * mo) * (g * (lo - l) + hl)

    mraw_f = lambda x: mraw[x].astype(F32)

    def convert(x, carry, put, ends):
        put(comb, (MASK, x + 1), mraw_f(x))
        return carry

    x_loop(8, convert, 0)
    zero = jnp.zeros((CY, CZ), F32)
    inside = lambda cond: jnp.where(cond, 1.0, 0.0).astype(F32)
    own_up_y, own_down_y = inside(row < CY - 1), inside(row > 0)
    own_up_z, own_down_z = inside(lane < CZ - 1), inside(lane > 0)

    def around(value):
        return (
            pltpu.roll(value, CY - 1, 0), pltpu.roll(value, 1, 0),
            pltpu.roll(value, CZ - 1, 1), pltpu.roll(value, 1, 1),
        )

    def before(x, carry, put, ends):
        first, second = carry
        a = lax.rem(gx + x // (CX // 2), GX)
        picked = []
        for half in range(2):
            b = lax.rem(gy + half, GY)
            table = jnp.broadcast_to(heatv[pl.ds(a * 4 + b // 4, 1), :], (8, CZ))
            index = jnp.bitwise_and(idv[x, half * 8 : half * 8 + 8, :], CZ - 1)
            picked.append(jnp.take_along_axis(table, index, axis=1))
        h = jnp.concatenate(picked, axis=0)
        put(hv, x, h)
        m, l, t = comb[MASK, x + 1], comb[LAM, x + 1], comb[TEMP, x + 1]
        hl = h * l
        above, below = jnp.minimum(x + 2, CX), jnp.maximum(x, 1)
        ms = (comb[MASK, above] * inside(x < CX - 1), comb[MASK, below] * inside(x > 0))
        my = around(m)
        ms += (my[0] * own_up_y, my[1] * own_down_y, my[2] * own_up_z, my[3] * own_down_z)
        ls = (comb[LAM, above], comb[LAM, below]) + around(l)
        ts = (comb[TEMP, above], comb[TEMP, below]) + around(t)
        base, half_t = 1.0 + 0.75 * (t * t), 0.5 * t
        added = -6.0 * hl
        for mo, lo, to in zip(ms, ls, ts):
            added = added + mo * ((base + to * (0.25 * to - half_t)) * (lo - l) + hl)
        part = l + (time_step * m) * added
        put(comb, (PART, x + 1), part)
        put(comb, (HEAT, x + 1), hl)
        put(tot, x, (t - ambient) * l)
        t1 = tpad[1, x + 1, ins, :]
        for f, value in enumerate((m, l, t, part, hl, t1, h)):
            put(ysend, (0, f, pl.ds(x, 1), slice(None)), value[:1])
            put(ysend, (1, f, pl.ds(x, 1), slice(None)), value[CY - 1 :])
        for f, value in enumerate((m, l, t, part)):
            first = jnp.where(lane == x + 32 * f, to_lane(value, x + 32 * f), first)
        for f, value in enumerate((hl, t1, tpad[0, x + 1, ins, :], h)):
            second = jnp.where(lane == x + 32 * f, to_lane(value, x + 32 * f), second)
        return first, second

    first, second = x_loop(4, before, (zero, zero))
    zsend[0] = first
    zsend[1] = second

    b0, b1 = gy, lax.rem(gy + 1, GY)
    low8 = lax.rem(lane8 // 32, 2) == 0
    s16 = jnp.zeros((GX, CZ), jnp.int32)
    for yh, b in enumerate((b0, b1)):
        those = ownv[pl.ds(b // 4, GX, stride=4), :]
        for c in range(2):
            shift = lax.rem(2 * CZ + 48 * c + 16 * yh - 32 * lax.rem(b, 4), CZ)
            here_it_is = (lane // 64 == c) & (lax.rem(lane // 16, 2) == yh)
            s16 = jnp.where(here_it_is, pltpu.roll(those, shift, 1), s16)
    slots = jnp.where(low8, s16[:8], pltpu.roll(s16[8:], 32, 1))

    pl.semaphore_wait(barrier, len(near))

    counter = [0]

    def remote(src, dst, device):
        i = counter[0]
        counter[0] += 1
        copy = pltpu.make_async_remote_copy(
            src_ref=src, dst_ref=dst, send_sem=ssem.at[i], recv_sem=rsem.at[i],
            device_id=device, device_id_type=MESH,
        )
        copy.start()
        return copy

    def x_faces(ref):
        return [
            remote(ref.at[CX, ins], ref.at[0, ins], at(1, 0, 0)),
            remote(ref.at[1, ins], ref.at[CX + 1, ins], at(-1, 0, 0)),
        ]

    def y_faces(ref):
        xs = pl.ds(1, CX)
        return [
            remote(ref.at[xs, pl.ds(Y0 + CY - 1, 1)], ref.at[xs, pl.ds(Y0 - 1, 1)], at(0, 1, 0)),
            remote(ref.at[xs, pl.ds(Y0, 1)], ref.at[xs, pl.ds(Y0 + CY, 1)], at(0, -1, 0)),
        ]

    sent = []

    def landed(copies):
        sent.extend(copies)
        for c in copies:
            c.wait_recv()

    three, five = pl.ds(0, 3), pl.ds(0, 5)
    round_1 = []
    for s, dx in ((0, 1), (1, -1)):
        for t, dy in ((0, 1), (1, -1)):
            x, y = (CX - 1 if dx == 1 else 0), (1 if dy == 1 else 0)
            round_1.append(remote(
                ysend.at[y, three, pl.ds(x, 1)], corner.at[s, t, three, pl.ds(0, 1)], at(dx, dy, 0)
            ))
    round_1 += [
        remote(comb.at[:, CX], comb.at[:, 0], at(1, 0, 0)),
        remote(comb.at[:, 1], comb.at[:, CX + 1], at(-1, 0, 0)),
        remote(zsend.at[0], zx.at[0], at(1, 0, 1)),
        remote(zsend.at[0], zx.at[1], at(-1, 0, 1)),
        remote(zsend.at[0], zy.at[0], at(0, 1, 1)),
        remote(zsend.at[0], zy.at[1], at(0, -1, 1)),
        remote(zsend.at[pl.ds(0, 2)], zrecv.at[pl.ds(0, 2)], at(0, 0, 1)),
        remote(ysend.at[1, five], yrecv.at[0, five], at(0, 1, 0)),
        remote(ysend.at[0, five], yrecv.at[1, five], at(0, -1, 0)),
    ]
    later_1 = x_faces(tpad.at[1]) + [
        remote(ysend.at[1, NEXT], yrecv.at[0, NEXT], at(0, 1, 0)),
        remote(ysend.at[0, NEXT], yrecv.at[1, NEXT], at(0, -1, 0)),
    ]
    for r in (4, -4):
        pl.semaphore_signal(zsem, inc=1, device_id=in_column(r), device_id_type=MESH)

    place = lax.rem(slots, PATCH_PER)
    which = lax.broadcasted_iota(jnp.int32, (CZ, CZ), 0)
    for r in range(8):
        hit = jnp.where(place[r : r + 1] == which, 1.0, 0.0)
        marks[r * CZ : (r + 1) * CZ, :] = jnp.transpose(hit).astype(jnp.bfloat16)

    def prepare_1(x, carry, put, ends):
        m, t, h = comb[MASK, x + 1], tpad[1, x + 1, ins, :], hv[x]
        above, below = jnp.minimum(x + 2, CX), jnp.maximum(x, 1)
        my = around(m)
        ms = (
            comb[MASK, above] * inside(x < CX - 1), comb[MASK, below] * inside(x > 0),
            my[0] * own_up_y, my[1] * own_down_y, my[2] * own_up_z, my[3] * own_down_z,
        )
        ts = (tpad[1, above, ins, :], tpad[1, below, ins, :]) + around(t)
        base, half_t = 1.0 + 0.75 * (t * t), 0.5 * t
        scaled, active = time_step * m, zero
        total = zero
        for d, (mo, to) in enumerate(zip(ms, ts)):
            k = (scaled * mo) * (base + to * (0.25 * to - half_t))
            active = active + mo
            total = total + k
            put(kk, (d, x), k)
        surface = scaled * (6.0 - active)
        put(kk, (6, x), 1.0 - surface * h - total)
        put(pe, x, surface)
        return carry

    x_loop(4, prepare_1, 0)
    landed(round_1)

    keep_x = (inside(gx > 0), inside(gx < GX - 1))
    keep_y = (inside(gy > 0), inside(gy < GY - 1))
    first_row, last_row = row == 0, row == CY - 1
    at_edge = inside(lane == edge)

    for s in range(2):
        mine, outer = (1, 0) if s == 0 else (CX, CX + 1)
        o = [comb[f, mine] for f in (MASK, LAM, TEMP, HEAT)]
        v = [comb[f, outer] for f in (MASK, LAM, TEMP, HEAT)]
        v[0] = v[0] * keep_x[s]
        xcor[s] = contribution(o, v[:3])
        new = comb[PART, outer] + contribution(v, o[:3])
        w = [jnp.where(first_row, corner[s, 0, f, :1, :], corner[s, 1, f, :1, :]) for f in range(3)]
        w[0] = w[0] * jnp.where(first_row, keep_y[0], jnp.where(last_row, keep_y[1], 0.0))
        new = new + contribution(v, w)
        source = CX - 1 if s == 0 else 0
        w = [from_lane(zx[s], 32 * f + source) for f in range(3)]
        w[0] = w[0] * at_edge
        l2[outer] = new + contribution(v, w)

    first_x, last_x = row32 == 0, row32 == CX - 1
    at_edge32 = inside(lane32 == edge)
    for t in range(2):
        o = [ysend[t, f] for f in (MASK, LAM, TEMP, HEAT)]
        v = [yrecv[t, f] for f in (MASK, LAM, TEMP, HEAT)]
        v[0] = v[0] * keep_y[t]
        ycor[t] = contribution(o, v[:3])
        new = yrecv[t, PART] + contribution(v, o[:3])
        w = [jnp.where(first_x, corner[0, t, f, :1, :], corner[1, t, f, :1, :]) for f in range(3)]
        w[0] = w[0] * jnp.where(first_x, keep_x[0], jnp.where(last_x, keep_x[1], 0.0))
        new = new + contribution(v, w)
        line = jnp.broadcast_to(zy[t, CY - 1 :, :] if t == 0 else zy[t, :1, :], (CX, CZ))
        w = [
            jnp.sum(jnp.where(lane32 == row32 + 32 * f, line, 0.0), axis=1, keepdims=True)
            for f in range(3)
        ]
        w = [jnp.broadcast_to(c, (CX, CZ)) for c in w]
        w[0] = w[0] * at_edge32
        l2y[t] = new + contribution(v, w)

    def group(packed, f):
        return packed if f == 0 else pltpu.roll(packed, CZ - 32 * f, 1)

    def moved(packed, source, target):
        shift = (target - source) % CZ
        return packed if shift == 0 else pltpu.roll(packed, shift, 1)

    o = [group(zsend[0], f) for f in range(3)] + [zsend[1]]
    v = [group(zrecv[0], f) for f in range(3)] + [zrecv[1]]
    zwork[0] = contribution(o, v[:3])
    new = group(zrecv[0], 3) + contribution(v, o[:3])
    w = [
        jnp.where(lane == 0, moved(zx[0], 32 * f + CX - 1, 0), moved(zx[1], 32 * f, CX - 1))
        for f in range(3)
    ]
    w[0] = w[0] * jnp.where(lane == 0, keep_x[0], jnp.where(lane == CX - 1, keep_x[1], 0.0))
    new = new + contribution(v, w)
    w = [
        jnp.where(first_row, group(zy[0, CY - 1 :, :], f), group(zy[1, :1, :], f))
        for f in range(3)
    ]
    w[0] = w[0] * jnp.where(first_row, keep_y[0], jnp.where(last_row, keep_y[1], 0.0))
    zwork[1] = new + contribution(v, w)

    def faces_of(x, refs, ends):
        xref, yref, zref = refs
        out = from_lane(zref[...], x) * at_edge
        out = out + jnp.where(
            first_row, yref[0, pl.ds(x, 1), :], jnp.where(last_row, yref[1, pl.ds(x, 1), :], 0.0)
        )
        if ends[0]:
            out = out + xref[0] * inside(x == 0)
        if ends[1]:
            out = out + xref[1] * inside(x == CX - 1)
        return out

    def finish_1(x, packed, put, ends):
        new = comb[PART, x + 1] + faces_of(x, (xcor, ycor, zwork.at[0]), ends)
        put(l2, x + 1, new)
        put(yl2, (0, pl.ds(x, 1), slice(None)), new[:1])
        put(yl2, (1, pl.ds(x, 1), slice(None)), new[CY - 1 :])
        return jnp.where(lane == x, to_lane(new, x), packed)

    zl2 = x_loop(16, finish_1, zero)
    landed(later_1)

    for s in range(2):
        mine, outer = (1, 0) if s == 0 else (CX, CX + 1)
        l = l2[mine]
        m, mo = comb[MASK, mine], comb[MASK, outer] * keep_x[s]
        xcor[s] = contribution(
            (m, l, tpad[1, mine, ins, :], hv[mine - 1] * l), (mo, l2[outer], tpad[1, outer, ins, :])
        )
        xpe[s] = -time_step * (m * mo)
    for t in range(2):
        l = yl2[t]
        m, mo = ysend[t, MASK], yrecv[t, MASK] * keep_y[t]
        ycor[t] = contribution(
            (m, l, ysend[t, NEXT], ysend[t, COEFF] * l), (mo, l2y[t], yrecv[t, NEXT])
        )
        ype[t] = -time_step * (m * mo)
    m, mo = zsend[0], zrecv[0]
    zwork[0] = contribution(
        (m, zl2, group(zsend[1], 1), group(zsend[1], 3) * zl2), (mo, zwork[1], group(zrecv[1], 1))
    )
    zwork[2] = -time_step * (m * mo)

    def z_neighbours(value, halo):
        up = jnp.where(lane == CZ - 1, halo, pltpu.roll(value, CZ - 1, 1))
        down = jnp.where(lane == 0, halo, pltpu.roll(value, 1, 1))
        return [up, down]

    def y_neighbours(value, up, down):
        return [
            jnp.where(last_row, up, pltpu.roll(value, CY - 1, 0)),
            jnp.where(first_row, down, pltpu.roll(value, 1, 0)),
        ]

    def six(ref, x, halo):
        here = ref[x + 1, ins, :]
        return here, [
            ref[x + 2, ins, :], ref[x, ins, :],
            ref[x + 1, pl.ds(Y0 + 1, CY), :], ref[x + 1, pl.ds(Y0 - 1, CY), :],
        ] + z_neighbours(here, halo)

    def masks(x):
        centre = comb[MASK, x + 1]
        up, down = z_neighbours(centre, from_lane(zrecv[0], x))
        others = [
            comb[MASK, x + 2] * inside((x < CX - 1) | (gx < GX - 1)),
            comb[MASK, x] * inside((x > 0) | (gx > 0)),
        ]
        others += y_neighbours(
            centre, yrecv[1, MASK, pl.ds(x, 1), :] * keep_y[1], yrecv[0, MASK, pl.ds(x, 1), :] * keep_y[0]
        )
        others += [
            up * jnp.where(lane == CZ - 1, inside(gz == 0), 1.0),
            down * jnp.where(lane == 0, inside(gz == 1), 1.0),
        ]
        active = others[0]
        for m in others[1:]:
            active = active + m
        scaled = time_step * centre
        surface = scaled * (6.0 - active)
        return [scaled * m for m in others], surface

    def coefficients(level, x, halo, faces, surface):
        here, there = six(tpad.at[level], x, halo)
        base = 1.0 + 0.75 * (here * here)
        half = 0.5 * here
        centre = 1.0 - surface * hv[x]
        out = []
        for t, m in zip(there, faces):
            k = m * (base + t * (0.25 * t - half))
            centre = centre - k
            out.append(k)
        return out, centre, here

    def apply(here, there, out, centre):
        new = centre * here
        for k, l in zip(out, there):
            new = new + k * l
        return new

    def step_2(x, packed, put, ends):
        here = l2[x + 1]
        there = (l2[x + 2], l2[x]) + around(here)
        new = apply(here, there, [kk[d, x] for d in range(6)], kk[6, x])
        new = new + faces_of(x, (xcor, ycor, zwork.at[0]), ends)
        surface = pe[x] + faces_of(x, (xpe, ype, zwork.at[2]), ends)
        put(lpad, (x + 1, ins, slice(None)), new)
        t0, t1 = tpad[0, x + 1, ins, :], tpad[1, x + 1, ins, :]
        put(tot, x, -surface * (tot[x] + (t1 - ambient) * here + (t0 - ambient) * new))
        return jnp.where(lane == x, to_lane(new, x), packed)

    zsend[2] = x_loop(16, step_2, zero)

    for xh in range(2):
        def gather(i, accs):
            for k in range(4):
                x = xh * (CX // 2) + 4 * i + k
                value = tot[x]
                offset = jnp.bitwise_and(idv[x], PATCH_PER - 1)
                accs = [acc + jnp.where(offset == o, value, 0.0) for o, acc in enumerate(accs)]
            return accs

        accs = lax.fori_loop(0, CX // 8, gather, [zero] * PATCH_PER)
        for yh in range(2):
            for o in range(PATCH_PER):
                accr[pl.ds(((xh * 2 + yh) * PATCH_PER + o) * 8, 8), :] = accs[o][yh * 8 : yh * 8 + 8]
    folded = [accr[pl.ds(i, 4 * PATCH_PER, stride=8), :] for i in range(8)]
    while len(folded) > 1:
        folded = [a + b for a, b in zip(folded[::2], folded[1::2])]
    turned = jnp.transpose(folded[0])
    halves = []
    for half in range(2):
        parts = [turned[half * 64 + i * 8 : half * 64 + i * 8 + 8] for i in range(8)]
        while len(parts) > 1:
            parts = [a + b for a, b in zip(parts[::2], parts[1::2])]
        halves.append(parts[0])
    by_cell = [jnp.where(gz == c, halves[0], halves[1]) for c in range(2)]
    message = jnp.concatenate([jnp.sum(v, axis=0, keepdims=True) for v in by_cell], axis=1)
    arow[0:1, :] = message

    own_row = gz * GX + gx
    for d in plane_peers:
        pltpu.make_async_remote_copy(
            src_ref=arow.at[pl.ds(0, 1)], dst_ref=plane.at[pl.ds(own_row, 1)],
            send_sem=gsem.at[0], recv_sem=gsem.at[1],
            device_id=in_plane(*d), device_id_type=MESH,
        ).start()
    round_3 = x_faces(lpad) + y_faces(lpad) + [remote(zsend.at[2], zrecv.at[2], at(0, 0, 1))]
    round_3 += x_faces(tpad.at[0]) + y_faces(tpad.at[0])

    count = pl.ds(0, GX * GZ - 1)
    pltpu.make_async_copy(plane.at[count], plane.at[count], gsem.at[1]).wait()
    sums = jnp.where(row32 == own_row, message, plane[...])
    sums = sums[:GX] + sums[GX:]
    shifted = pltpu.roll(sums, CZ - 32, 1)
    sums = sums + jnp.concatenate([shifted[GX - 1 :], shifted[: GX - 1]], axis=0)
    sums = jnp.where(low8, sums[:8], pltpu.roll(sums[8:], 32, 1))

    mine = jnp.where((slots // 512 == gx) & (lax.rem(slots // 16, 2) == gz), sums, 0.0)
    target = lax.rem(slots // 32, GY)
    values = [jnp.where(target[r : r + 1] == row, mine[r : r + 1], 0.0) for r in range(8)]
    rest = jnp.concatenate(values, axis=1)
    pieces = []
    for _ in range(3):
        pieces.append(rest.astype(jnp.bfloat16))
        rest = rest - pieces[-1].astype(F32)
    share = lax.dot_general(
        jnp.concatenate(pieces, axis=0), marks[...], (((1,), (0,)), ((), ())),
        preferred_element_type=F32,
    )
    share = share[:GY] + share[GY : 2 * GY] + share[2 * GY :]
    rrow[...] = share
    pl.semaphore_wait(zsem, 2)
    for r in column_peers:
        to = in_column(r)
        pltpu.make_async_remote_copy(
            src_ref=rrow.at[pl.ds(to[1], 1)], dst_ref=zbuf.at[pl.ds(gy, 1)],
            send_sem=gsem.at[2], recv_sem=gsem.at[3],
            device_id=to, device_id_type=MESH,
        ).start()

    landed(round_3)

    def step_3(x, carry, put, ends):
        out, centre, _ = coefficients(0, x, from_lane(zrecv[1], x + 64), *masks(x))
        here, there = six(lpad, x, from_lane(zrecv[2], x))
        put(sens, x, apply(here, there, out, centre))
        return carry

    x_loop(4, step_3, 0)
    for c in sent:
        c.wait_send()
    pltpu.make_async_copy(plane.at[count], plane.at[count], gsem.at[0]).wait()
    count = pl.ds(0, GY - 1)
    pltpu.make_async_copy(zbuf.at[count], zbuf.at[count], gsem.at[3]).wait()
    final = jnp.where(row == gy, share, zbuf[...])
    patch[...] = jnp.sum(final, axis=0)[:PATCH_PER]
    pltpu.make_async_copy(zbuf.at[count], zbuf.at[count], gsem.at[2]).wait()


def on_device(temps, cotangent, solid_mask, patch_ids, heat_coeff, owner_slot):
    anywhere = pl.BlockSpec(memory_space=pltpu.HBM)
    vmem = pl.BlockSpec(memory_space=pltpu.VMEM)
    field = (CX, CY, CZ)
    copies = 13 + 4 * 2 + 5
    sens, patch = pl.pallas_call(
        kernel,
        name="adjoint",
        out_shape=(
            pltpu.VMEM(field, F32),
            pltpu.VMEM((PATCH_PER,), F32),
        ),
        in_specs=[anywhere] * 6,
        out_specs=(vmem, vmem),
        scratch_shapes=[
            pltpu.VMEM((5, CX + 2, CY, CZ), F32),
            pltpu.VMEM((2, CX + 2, CY + 16, CZ), F32),
            pltpu.VMEM((CX + 2, CY, CZ), F32),
            pltpu.VMEM((CX + 2, CY + 16, CZ), F32),
            pltpu.VMEM(field, jnp.int32),
            pltpu.VMEM(field, jnp.int32),
            pltpu.VMEM((64, CZ), F32),
            pltpu.VMEM((64, CZ), jnp.int32),
            pltpu.VMEM(field, F32),
            pltpu.VMEM((7,) + field, F32),
            pltpu.VMEM(field, F32),
            pltpu.VMEM(field, F32),
            pltpu.VMEM((2, 7, CX, CZ), F32),
            pltpu.VMEM((2, 6, CX, CZ), F32),
            pltpu.VMEM((2, 2, 3, 8, CZ), F32),
            pltpu.VMEM((2, CX, CZ), F32),
            pltpu.VMEM((2, CX, CZ), F32),
            pltpu.VMEM((2, CX, CZ), F32),
            pltpu.VMEM((2, CX, CZ), F32),
            pltpu.VMEM((2, CY, CZ), F32),
            pltpu.VMEM((2, CY, CZ), F32),
            pltpu.VMEM((3, CY, CZ), F32),
            pltpu.VMEM((3, CY, CZ), F32),
            pltpu.VMEM((2, CY, CZ), F32),
            pltpu.VMEM((2, CY, CZ), F32),
            pltpu.VMEM((3, CY, CZ), F32),
            pltpu.VMEM((64 * 8, CZ), F32),
            pltpu.VMEM((8 * CZ, CZ), jnp.bfloat16),
            pltpu.VMEM((8, CZ), F32),
            pltpu.VMEM((GX * GZ, CZ), F32),
            pltpu.VMEM((GY, CZ), F32),
            pltpu.VMEM((GY, CZ), F32),
            pltpu.SemaphoreType.DMA((8,)),
            pltpu.SemaphoreType.DMA((copies,)),
            pltpu.SemaphoreType.DMA((copies,)),
            pltpu.SemaphoreType.DMA((4,)),
            pltpu.SemaphoreType.REGULAR,
        ],
        compiler_params=pltpu.CompilerParams(
            collective_id=0, has_side_effects=True, vmem_limit_bytes=60 * 1024 * 1024
        ),
    )(
        temps, cotangent, solid_mask, patch_ids,
        heat_coeff.reshape(64, CZ), owner_slot.reshape(64, CZ),
    )
    return sens, patch


def solution(mesh):
    placed = (
        P(None, "gx", "gy", "gz"),
        P("gx", "gy", "gz"),
        P("gx", "gy", "gz"),
        P("gx", "gy", "gz"),
        P(),
        P(),
    )
    return jax.shard_map(
        on_device,
        mesh=mesh,
        in_specs=placed,
        out_specs=(P("gx", "gy", "gz"), P(("gx", "gy", "gz"))),
        check_vma=False,
    )
```

```python
import jax
import jax.numpy as jnp
from jax import lax
from jax.experimental import pallas as pl
from jax.experimental.pallas import tpu as pltpu
from jax.sharding import PartitionSpec as P

STEPS = 3
PATCH_PER = 16
GX, GY, GZ = 16, 16, 2
CX, CY, CZ = 32, 16, 128
Y0 = 8
F32 = jnp.float32
MESH = pl.DeviceIdType.MESH

time_step = 0.12
ambient = 0.6


def x_loop(unroll, body, init):
    def block(i, carry):
        stores = []
        for k in range(unroll):
            ends = (k == 0, k == unroll - 1)
            carry = body(i * unroll + k, carry, lambda *store: stores.append(store), ends)
        for ref, index, value in stores:
            ref[index] = value
        return carry

    return lax.fori_loop(0, CX // unroll, block, init)


MASK, LAM, TEMP, PART, HEAT = range(5)
NEXT, COEFF = 5, 6


def kernel(
    temps, cot, mask, ids, heat, owner,
    sens, patch,
    comb, tpad, l2, lpad, mraw, idv, heatv, ownv, hv, kk, pe, tot,
    ysend, yrecv, corner, ycor, ype, yl2, l2y, xcor, xpe,
    zsend, zrecv, zx, zy, zwork, accr, marks, arow, plane, rrow, zbuf,
    lsem, ssem, rsem, gsem, zsem,
):
    gx, gy, gz = lax.axis_index("gx"), lax.axis_index("gy"), lax.axis_index("gz")

    def in_plane(dx, dy, dc):
        x, y = lax.rem(gx // 4 + dx, 4), lax.rem(lax.rem(gx // 2, 2) * 2 + gz + dy, 4)
        return (x * 4 + y // 2 * 2 + lax.rem(gx + dc, 2), gy, lax.rem(y, 2))

    hops = lambda n, size: min(n, size - n)
    plane_peers = [(dx, dy, dc) for dx in range(4) for dy in range(4) for dc in range(2)][1:]
    plane_peers.sort(key=lambda d: -hops(d[0], 4) - hops(d[1], 4))
    column_peers = sorted(range(1, GY), key=lambda r: -hops(r, GY))

    def at(dx, dy, dz):
        return (lax.rem(gx + dx + GX, GX), lax.rem(gy + dy + GY, GY), 1 - gz if dz else gz)

    def in_column(r):
        return at(0, r, 0)

    barrier = pltpu.get_barrier_semaphore()
    near = [at(dx, dy, 0) for dx in (1, -1) for dy in (1, -1)]
    near += [in_plane(*d) for d in plane_peers[:10]]
    near += [in_column(r) for r in (4, -4, 3, -3, 2, -2, 1, -1)]
    near += [at(0, dy, 1) for dy in (1, -1)]
    near += [in_plane(*d) for d in plane_peers[10:]]
    for device in near:
        pl.semaphore_signal(barrier, inc=1, device_id=device, device_id_type=MESH)

    inner = (pl.ds(1, CX), pl.ds(Y0, CY))
    loads = [
        (mask, mraw), (cot, comb.at[LAM, pl.ds(1, CX)]), (temps.at[2], comb.at[TEMP, pl.ds(1, CX)]),
        (ids, idv), (heat, heatv), (owner, ownv),
        (temps.at[1], tpad.at[1].at[inner]),
        (temps.at[0], tpad.at[0].at[inner]),
    ]
    loads = [pltpu.make_async_copy(s, d, lsem.at[i]) for i, (s, d) in enumerate(loads)]
    for c in loads:
        c.start()
    for c in loads:
        c.wait()

    lane = lax.broadcasted_iota(jnp.int32, (CY, CZ), 1)
    row = lax.broadcasted_iota(jnp.int32, (CY, CZ), 0)
    lane8 = lax.broadcasted_iota(jnp.int32, (8, CZ), 1)
    lane32 = lax.broadcasted_iota(jnp.int32, (CX, CZ), 1)
    row32 = lax.broadcasted_iota(jnp.int32, (CX, CZ), 0)
    edge = jnp.where(gz == 0, CZ - 1, 0)
    ins = pl.ds(Y0, CY)

    def to_lane(value, target):
        return pltpu.roll(value, lax.rem(target - edge + CZ, CZ), 1)

    def from_lane(packed, source):
        return pltpu.roll(packed, lax.rem(edge - source + CZ, CZ), 1)

    def contribution(one, other):
        m, l, t, hl = one
        mo, lo, to = other
        g = 1.0 + 0.75 * (t * t) + to * (0.25 * to - 0.5 * t)
        return time_step * (m * mo) * (g * (lo - l) + hl)

    mraw_f = lambda x: mraw[x].astype(F32)

    def convert(x, carry, put, ends):
        put(comb, (MASK, x + 1), mraw_f(x))
        return carry

    x_loop(8, convert, 0)
    zero = jnp.zeros((CY, CZ), F32)
    inside = lambda cond: jnp.where(cond, 1.0, 0.0).astype(F32)
    own_up_y, own_down_y = inside(row < CY - 1), inside(row > 0)
    own_up_z, own_down_z = inside(lane < CZ - 1), inside(lane > 0)

    def around(value):
        return (
            pltpu.roll(value, CY - 1, 0), pltpu.roll(value, 1, 0),
            pltpu.roll(value, CZ - 1, 1), pltpu.roll(value, 1, 1),
        )

    def before(x, carry, put, ends):
        first, second = carry
        a = lax.rem(gx + x // (CX // 2), GX)
        picked = []
        for half in range(2):
            b = lax.rem(gy + half, GY)
            table = jnp.broadcast_to(heatv[pl.ds(a * 4 + b // 4, 1), :], (8, CZ))
            index = jnp.bitwise_and(idv[x, half * 8 : half * 8 + 8, :], CZ - 1)
            picked.append(jnp.take_along_axis(table, index, axis=1))
        h = jnp.concatenate(picked, axis=0)
        put(hv, x, h)
        m, l, t = comb[MASK, x + 1], comb[LAM, x + 1], comb[TEMP, x + 1]
        hl = h * l
        above, below = jnp.minimum(x + 2, CX), jnp.maximum(x, 1)
        ms = (comb[MASK, above] * inside(x < CX - 1), comb[MASK, below] * inside(x > 0))
        my = around(m)
        ms += (my[0] * own_up_y, my[1] * own_down_y, my[2] * own_up_z, my[3] * own_down_z)
        ls = (comb[LAM, above], comb[LAM, below]) + around(l)
        ts = (comb[TEMP, above], comb[TEMP, below]) + around(t)
        base, half_t = 1.0 + 0.75 * (t * t), 0.5 * t
        added = -6.0 * hl
        for mo, lo, to in zip(ms, ls, ts):
            added = added + mo * ((base + to * (0.25 * to - half_t)) * (lo - l) + hl)
        part = l + (time_step * m) * added
        put(comb, (PART, x + 1), part)
        put(comb, (HEAT, x + 1), hl)
        put(tot, x, (t - ambient) * l)
        t1 = tpad[1, x + 1, ins, :]
        for f, value in enumerate((m, l, t, part, hl, t1, h)):
            put(ysend, (0, f, pl.ds(x, 1), slice(None)), value[:1])
            put(ysend, (1, f, pl.ds(x, 1), slice(None)), value[CY - 1 :])
        for f, value in enumerate((m, l, t, part)):
            first = jnp.where(lane == x + 32 * f, to_lane(value, x + 32 * f), first)
        for f, value in enumerate((hl, t1, tpad[0, x + 1, ins, :], h)):
            second = jnp.where(lane == x + 32 * f, to_lane(value, x + 32 * f), second)
        return first, second

    first, second = x_loop(4, before, (zero, zero))
    zsend[0] = first
    zsend[1] = second

    b0, b1 = gy, lax.rem(gy + 1, GY)
    low8 = lax.rem(lane8 // 32, 2) == 0
    s16 = jnp.zeros((GX, CZ), jnp.int32)
    for yh, b in enumerate((b0, b1)):
        those = ownv[pl.ds(b // 4, GX, stride=4), :]
        for c in range(2):
            shift = lax.rem(2 * CZ + 48 * c + 16 * yh - 32 * lax.rem(b, 4), CZ)
            here_it_is = (lane // 64 == c) & (lax.rem(lane // 16, 2) == yh)
            s16 = jnp.where(here_it_is, pltpu.roll(those, shift, 1), s16)
    slots = jnp.where(low8, s16[:8], pltpu.roll(s16[8:], 32, 1))

    pl.semaphore_wait(barrier, len(near))

    counter = [0]

    def remote(src, dst, device):
        i = counter[0]
        counter[0] += 1
        copy = pltpu.make_async_remote_copy(
            src_ref=src, dst_ref=dst, send_sem=ssem.at[i], recv_sem=rsem.at[i],
            device_id=device, device_id_type=MESH,
        )
        copy.start()
        return copy

    def x_faces(ref):
        return [
            remote(ref.at[CX, ins], ref.at[0, ins], at(1, 0, 0)),
            remote(ref.at[1, ins], ref.at[CX + 1, ins], at(-1, 0, 0)),
        ]

    def y_faces(ref):
        xs = pl.ds(1, CX)
        return [
            remote(ref.at[xs, pl.ds(Y0 + CY - 1, 1)], ref.at[xs, pl.ds(Y0 - 1, 1)], at(0, 1, 0)),
            remote(ref.at[xs, pl.ds(Y0, 1)], ref.at[xs, pl.ds(Y0 + CY, 1)], at(0, -1, 0)),
        ]

    sent = []

    def landed(copies):
        sent.extend(copies)
        for c in copies:
            c.wait_recv()

    three, five = pl.ds(0, 3), pl.ds(0, 5)
    round_1 = [
        remote(comb.at[:, CX], comb.at[:, 0], at(1, 0, 0)),
        remote(comb.at[:, 1], comb.at[:, CX + 1], at(-1, 0, 0)),
    ]
    for s, dx in ((0, 1), (1, -1)):
        for t, dy in ((0, 1), (1, -1)):
            x, y = (CX - 1 if dx == 1 else 0), (1 if dy == 1 else 0)
            round_1.append(remote(
                ysend.at[y, three, pl.ds(x, 1)], corner.at[s, t, three, pl.ds(0, 1)], at(dx, dy, 0)
            ))
    round_1 += [
        remote(zsend.at[0], zx.at[0], at(1, 0, 1)),
        remote(zsend.at[0], zx.at[1], at(-1, 0, 1)),
        remote(zsend.at[0], zy.at[0], at(0, 1, 1)),
        remote(zsend.at[0], zy.at[1], at(0, -1, 1)),
        remote(zsend.at[pl.ds(0, 2)], zrecv.at[pl.ds(0, 2)], at(0, 0, 1)),
        remote(ysend.at[1, five], yrecv.at[0, five], at(0, 1, 0)),
        remote(ysend.at[0, five], yrecv.at[1, five], at(0, -1, 0)),
    ]
    later_1 = [
        x_faces(tpad.at[1]) + [
            remote(ysend.at[1, NEXT], yrecv.at[0, NEXT], at(0, 1, 0)),
            remote(ysend.at[0, NEXT], yrecv.at[1, NEXT], at(0, -1, 0)),
        ],
        x_faces(tpad.at[0]) + y_faces(tpad.at[0]),
    ]
    for r in (4, -4):
        pl.semaphore_signal(zsem, inc=1, device_id=in_column(r), device_id_type=MESH)

    place = lax.rem(slots, PATCH_PER)
    which = lax.broadcasted_iota(jnp.int32, (CZ, CZ), 0)
    for r in range(8):
        hit = jnp.where(place[r : r + 1] == which, 1.0, 0.0)
        marks[r * CZ : (r + 1) * CZ, :] = jnp.transpose(hit).astype(jnp.bfloat16)

    def prepare_1(x, carry, put, ends):
        m, t, h = comb[MASK, x + 1], tpad[1, x + 1, ins, :], hv[x]
        above, below = jnp.minimum(x + 2, CX), jnp.maximum(x, 1)
        my = around(m)
        ms = (
            comb[MASK, above] * inside(x < CX - 1), comb[MASK, below] * inside(x > 0),
            my[0] * own_up_y, my[1] * own_down_y, my[2] * own_up_z, my[3] * own_down_z,
        )
        ts = (tpad[1, above, ins, :], tpad[1, below, ins, :]) + around(t)
        base, half_t = 1.0 + 0.75 * (t * t), 0.5 * t
        scaled, active = time_step * m, zero
        total = zero
        for d, (mo, to) in enumerate(zip(ms, ts)):
            k = (scaled * mo) * (base + to * (0.25 * to - half_t))
            active = active + mo
            total = total + k
            put(kk, (d, x), k)
        surface = scaled * (6.0 - active)
        put(kk, (6, x), 1.0 - surface * h - total)
        put(pe, x, surface)
        return carry

    x_loop(4, prepare_1, 0)
    landed(round_1)

    keep_x = (inside(gx > 0), inside(gx < GX - 1))
    keep_y = (inside(gy > 0), inside(gy < GY - 1))
    first_row, last_row = row == 0, row == CY - 1
    at_edge = inside(lane == edge)

    for s in range(2):
        mine, outer = (1, 0) if s == 0 else (CX, CX + 1)
        o = [comb[f, mine] for f in (MASK, LAM, TEMP, HEAT)]
        v = [comb[f, outer] for f in (MASK, LAM, TEMP, HEAT)]
        v[0] = v[0] * keep_x[s]
        xcor[s] = contribution(o, v[:3])
        new = comb[PART, outer] + contribution(v, o[:3])
        w = [jnp.where(first_row, corner[s, 0, f, :1, :], corner[s, 1, f, :1, :]) for f in range(3)]
        w[0] = w[0] * jnp.where(first_row, keep_y[0], jnp.where(last_row, keep_y[1], 0.0))
        new = new + contribution(v, w)
        source = CX - 1 if s == 0 else 0
        w = [from_lane(zx[s], 32 * f + source) for f in range(3)]
        w[0] = w[0] * at_edge
        l2[outer] = new + contribution(v, w)

    first_x, last_x = row32 == 0, row32 == CX - 1
    at_edge32 = inside(lane32 == edge)
    for t in range(2):
        o = [ysend[t, f] for f in (MASK, LAM, TEMP, HEAT)]
        v = [yrecv[t, f] for f in (MASK, LAM, TEMP, HEAT)]
        v[0] = v[0] * keep_y[t]
        ycor[t] = contribution(o, v[:3])
        new = yrecv[t, PART] + contribution(v, o[:3])
        w = [jnp.where(first_x, corner[0, t, f, :1, :], corner[1, t, f, :1, :]) for f in range(3)]
        w[0] = w[0] * jnp.where(first_x, keep_x[0], jnp.where(last_x, keep_x[1], 0.0))
        new = new + contribution(v, w)
        line = jnp.broadcast_to(zy[t, CY - 1 :, :] if t == 0 else zy[t, :1, :], (CX, CZ))
        w = [
            jnp.sum(jnp.where(lane32 == row32 + 32 * f, line, 0.0), axis=1, keepdims=True)
            for f in range(3)
        ]
        w = [jnp.broadcast_to(c, (CX, CZ)) for c in w]
        w[0] = w[0] * at_edge32
        l2y[t] = new + contribution(v, w)

    def group(packed, f):
        return packed if f == 0 else pltpu.roll(packed, CZ - 32 * f, 1)

    def moved(packed, source, target):
        shift = (target - source) % CZ
        return packed if shift == 0 else pltpu.roll(packed, shift, 1)

    o = [group(zsend[0], f) for f in range(3)] + [zsend[1]]
    v = [group(zrecv[0], f) for f in range(3)] + [zrecv[1]]
    zwork[0] = contribution(o, v[:3])
    new = group(zrecv[0], 3) + contribution(v, o[:3])
    w = [
        jnp.where(lane == 0, moved(zx[0], 32 * f + CX - 1, 0), moved(zx[1], 32 * f, CX - 1))
        for f in range(3)
    ]
    w[0] = w[0] * jnp.where(lane == 0, keep_x[0], jnp.where(lane == CX - 1, keep_x[1], 0.0))
    new = new + contribution(v, w)
    w = [
        jnp.where(first_row, group(zy[0, CY - 1 :, :], f), group(zy[1, :1, :], f))
        for f in range(3)
    ]
    w[0] = w[0] * jnp.where(first_row, keep_y[0], jnp.where(last_row, keep_y[1], 0.0))
    zwork[1] = new + contribution(v, w)

    def faces_of(x, refs, ends):
        xref, yref, zref = refs
        out = from_lane(zref[...], x) * at_edge
        out = out + jnp.where(
            first_row, yref[0, pl.ds(x, 1), :], jnp.where(last_row, yref[1, pl.ds(x, 1), :], 0.0)
        )
        if ends[0]:
            out = out + xref[0] * inside(x == 0)
        if ends[1]:
            out = out + xref[1] * inside(x == CX - 1)
        return out

    def finish_1(x, packed, put, ends):
        new = comb[PART, x + 1] + faces_of(x, (xcor, ycor, zwork.at[0]), ends)
        put(l2, x + 1, new)
        put(yl2, (0, pl.ds(x, 1), slice(None)), new[:1])
        put(yl2, (1, pl.ds(x, 1), slice(None)), new[CY - 1 :])
        return jnp.where(lane == x, to_lane(new, x), packed)

    zl2 = x_loop(16, finish_1, zero)
    landed(later_1[0])

    for s in range(2):
        mine, outer = (1, 0) if s == 0 else (CX, CX + 1)
        l = l2[mine]
        m, mo = comb[MASK, mine], comb[MASK, outer] * keep_x[s]
        xcor[s] = contribution(
            (m, l, tpad[1, mine, ins, :], hv[mine - 1] * l), (mo, l2[outer], tpad[1, outer, ins, :])
        )
        xpe[s] = -time_step * (m * mo)
    for t in range(2):
        l = yl2[t]
        m, mo = ysend[t, MASK], yrecv[t, MASK] * keep_y[t]
        ycor[t] = contribution(
            (m, l, ysend[t, NEXT], ysend[t, COEFF] * l), (mo, l2y[t], yrecv[t, NEXT])
        )
        ype[t] = -time_step * (m * mo)
    m, mo = zsend[0], zrecv[0]
    zwork[0] = contribution(
        (m, zl2, group(zsend[1], 1), group(zsend[1], 3) * zl2), (mo, zwork[1], group(zrecv[1], 1))
    )
    zwork[2] = -time_step * (m * mo)

    def z_neighbours(value, halo):
        up = jnp.where(lane == CZ - 1, halo, pltpu.roll(value, CZ - 1, 1))
        down = jnp.where(lane == 0, halo, pltpu.roll(value, 1, 1))
        return [up, down]

    def y_neighbours(value, up, down):
        return [
            jnp.where(last_row, up, pltpu.roll(value, CY - 1, 0)),
            jnp.where(first_row, down, pltpu.roll(value, 1, 0)),
        ]

    def six(ref, x, halo):
        here = ref[x + 1, ins, :]
        return here, [
            ref[x + 2, ins, :], ref[x, ins, :],
            ref[x + 1, pl.ds(Y0 + 1, CY), :], ref[x + 1, pl.ds(Y0 - 1, CY), :],
        ] + z_neighbours(here, halo)

    def masks(x):
        centre = comb[MASK, x + 1]
        up, down = z_neighbours(centre, from_lane(zrecv[0], x))
        others = [
            comb[MASK, x + 2] * inside((x < CX - 1) | (gx < GX - 1)),
            comb[MASK, x] * inside((x > 0) | (gx > 0)),
        ]
        others += y_neighbours(
            centre, yrecv[1, MASK, pl.ds(x, 1), :] * keep_y[1], yrecv[0, MASK, pl.ds(x, 1), :] * keep_y[0]
        )
        others += [
            up * jnp.where(lane == CZ - 1, inside(gz == 0), 1.0),
            down * jnp.where(lane == 0, inside(gz == 1), 1.0),
        ]
        active = others[0]
        for m in others[1:]:
            active = active + m
        scaled = time_step * centre
        surface = scaled * (6.0 - active)
        return [scaled * m for m in others], surface

    def coefficients(level, x, halo, faces, surface):
        here, there = six(tpad.at[level], x, halo)
        base = 1.0 + 0.75 * (here * here)
        half = 0.5 * here
        centre = 1.0 - surface * hv[x]
        out = []
        for t, m in zip(there, faces):
            k = m * (base + t * (0.25 * t - half))
            centre = centre - k
            out.append(k)
        return out, centre, here

    def apply(here, there, out, centre):
        new = centre * here
        for k, l in zip(out, there):
            new = new + k * l
        return new

    def step_2(x, packed, put, ends):
        here = l2[x + 1]
        there = (l2[x + 2], l2[x]) + around(here)
        new = apply(here, there, [kk[d, x] for d in range(6)], kk[6, x])
        new = new + faces_of(x, (xcor, ycor, zwork.at[0]), ends)
        surface = pe[x] + faces_of(x, (xpe, ype, zwork.at[2]), ends)
        put(lpad, (x + 1, ins, slice(None)), new)
        t0, t1 = tpad[0, x + 1, ins, :], tpad[1, x + 1, ins, :]
        put(tot, x, -surface * (tot[x] + (t1 - ambient) * here + (t0 - ambient) * new))
        return jnp.where(lane == x, to_lane(new, x), packed)

    zsend[2] = x_loop(16, step_2, zero)

    for xh in range(2):
        def gather(i, accs):
            for k in range(4):
                x = xh * (CX // 2) + 4 * i + k
                value = tot[x]
                offset = jnp.bitwise_and(idv[x], PATCH_PER - 1)
                accs = [acc + jnp.where(offset == o, value, 0.0) for o, acc in enumerate(accs)]
            return accs

        accs = lax.fori_loop(0, CX // 8, gather, [zero] * PATCH_PER)
        for yh in range(2):
            for o in range(PATCH_PER):
                accr[pl.ds(((xh * 2 + yh) * PATCH_PER + o) * 8, 8), :] = accs[o][yh * 8 : yh * 8 + 8]
    folded = [accr[pl.ds(i, 4 * PATCH_PER, stride=8), :] for i in range(8)]
    while len(folded) > 1:
        folded = [a + b for a, b in zip(folded[::2], folded[1::2])]
    turned = jnp.transpose(folded[0])
    halves = []
    for half in range(2):
        parts = [turned[half * 64 + i * 8 : half * 64 + i * 8 + 8] for i in range(8)]
        while len(parts) > 1:
            parts = [a + b for a, b in zip(parts[::2], parts[1::2])]
        halves.append(parts[0])
    by_cell = [jnp.where(gz == c, halves[0], halves[1]) for c in range(2)]
    message = jnp.concatenate([jnp.sum(v, axis=0, keepdims=True) for v in by_cell], axis=1)
    arow[0:1, :] = message

    own_row = gz * GX + gx
    for d in plane_peers:
        pltpu.make_async_remote_copy(
            src_ref=arow.at[pl.ds(0, 1)], dst_ref=plane.at[pl.ds(own_row, 1)],
            send_sem=gsem.at[0], recv_sem=gsem.at[1],
            device_id=in_plane(*d), device_id_type=MESH,
        ).start()
    round_3 = x_faces(lpad) + y_faces(lpad) + [remote(zsend.at[2], zrecv.at[2], at(0, 0, 1))]
    landed(later_1[1])

    count = pl.ds(0, GX * GZ - 1)
    pltpu.make_async_copy(plane.at[count], plane.at[count], gsem.at[1]).wait()
    sums = jnp.where(row32 == own_row, message, plane[...])
    sums = sums[:GX] + sums[GX:]
    shifted = pltpu.roll(sums, CZ - 32, 1)
    sums = sums + jnp.concatenate([shifted[GX - 1 :], shifted[: GX - 1]], axis=0)
    sums = jnp.where(low8, sums[:8], pltpu.roll(sums[8:], 32, 1))

    mine = jnp.where((slots // 512 == gx) & (lax.rem(slots // 16, 2) == gz), sums, 0.0)
    target = lax.rem(slots // 32, GY)
    values = [jnp.where(target[r : r + 1] == row, mine[r : r + 1], 0.0) for r in range(8)]
    rest = jnp.concatenate(values, axis=1)
    pieces = []
    for _ in range(3):
        pieces.append(rest.astype(jnp.bfloat16))
        rest = rest - pieces[-1].astype(F32)
    share = lax.dot_general(
        jnp.concatenate(pieces, axis=0), marks[...], (((1,), (0,)), ((), ())),
        preferred_element_type=F32,
    )
    share = share[:GY] + share[GY : 2 * GY] + share[2 * GY :]
    rrow[...] = share
    pl.semaphore_wait(zsem, 2)
    for r in column_peers:
        to = in_column(r)
        pltpu.make_async_remote_copy(
            src_ref=rrow.at[pl.ds(to[1], 1)], dst_ref=zbuf.at[pl.ds(gy, 1)],
            send_sem=gsem.at[2], recv_sem=gsem.at[3],
            device_id=to, device_id_type=MESH,
        ).start()

    landed(round_3)

    def step_3(x, carry, put, ends):
        out, centre, _ = coefficients(0, x, from_lane(zrecv[1], x + 64), *masks(x))
        here, there = six(lpad, x, from_lane(zrecv[2], x))
        put(sens, x, apply(here, there, out, centre))
        return carry

    x_loop(4, step_3, 0)
    for c in sent:
        c.wait_send()
    pltpu.make_async_copy(plane.at[count], plane.at[count], gsem.at[0]).wait()
    count = pl.ds(0, GY - 1)
    pltpu.make_async_copy(zbuf.at[count], zbuf.at[count], gsem.at[3]).wait()
    final = jnp.where(row == gy, share, zbuf[...])
    patch[...] = jnp.sum(final, axis=0)[:PATCH_PER]
    pltpu.make_async_copy(zbuf.at[count], zbuf.at[count], gsem.at[2]).wait()


def on_device(temps, cotangent, solid_mask, patch_ids, heat_coeff, owner_slot):
    anywhere = pl.BlockSpec(memory_space=pltpu.HBM)
    vmem = pl.BlockSpec(memory_space=pltpu.VMEM)
    field = (CX, CY, CZ)
    copies = 13 + 4 * 2 + 5
    sens, patch = pl.pallas_call(
        kernel,
        name="adjoint",
        out_shape=(
            pltpu.VMEM(field, F32),
            pltpu.VMEM((PATCH_PER,), F32),
        ),
        in_specs=[anywhere] * 6,
        out_specs=(vmem, vmem),
        scratch_shapes=[
            pltpu.VMEM((5, CX + 2, CY, CZ), F32),
            pltpu.VMEM((2, CX + 2, CY + 16, CZ), F32),
            pltpu.VMEM((CX + 2, CY, CZ), F32),
            pltpu.VMEM((CX + 2, CY + 16, CZ), F32),
            pltpu.VMEM(field, jnp.int32),
            pltpu.VMEM(field, jnp.int32),
            pltpu.VMEM((64, CZ), F32),
            pltpu.VMEM((64, CZ), jnp.int32),
            pltpu.VMEM(field, F32),
            pltpu.VMEM((7,) + field, F32),
            pltpu.VMEM(field, F32),
            pltpu.VMEM(field, F32),
            pltpu.VMEM((2, 7, CX, CZ), F32),
            pltpu.VMEM((2, 6, CX, CZ), F32),
            pltpu.VMEM((2, 2, 3, 8, CZ), F32),
            pltpu.VMEM((2, CX, CZ), F32),
            pltpu.VMEM((2, CX, CZ), F32),
            pltpu.VMEM((2, CX, CZ), F32),
            pltpu.VMEM((2, CX, CZ), F32),
            pltpu.VMEM((2, CY, CZ), F32),
            pltpu.VMEM((2, CY, CZ), F32),
            pltpu.VMEM((3, CY, CZ), F32),
            pltpu.VMEM((3, CY, CZ), F32),
            pltpu.VMEM((2, CY, CZ), F32),
            pltpu.VMEM((2, CY, CZ), F32),
            pltpu.VMEM((3, CY, CZ), F32),
            pltpu.VMEM((64 * 8, CZ), F32),
            pltpu.VMEM((8 * CZ, CZ), jnp.bfloat16),
            pltpu.VMEM((8, CZ), F32),
            pltpu.VMEM((GX * GZ, CZ), F32),
            pltpu.VMEM((GY, CZ), F32),
            pltpu.VMEM((GY, CZ), F32),
            pltpu.SemaphoreType.DMA((8,)),
            pltpu.SemaphoreType.DMA((copies,)),
            pltpu.SemaphoreType.DMA((copies,)),
            pltpu.SemaphoreType.DMA((4,)),
            pltpu.SemaphoreType.REGULAR,
        ],
        compiler_params=pltpu.CompilerParams(
            collective_id=0, has_side_effects=True, vmem_limit_bytes=60 * 1024 * 1024
        ),
    )(
        temps, cotangent, solid_mask, patch_ids,
        heat_coeff.reshape(64, CZ), owner_slot.reshape(64, CZ),
    )
    return sens, patch


def solution(mesh):
    placed = (
        P(None, "gx", "gy", "gz"),
        P("gx", "gy", "gz"),
        P("gx", "gy", "gz"),
        P("gx", "gy", "gz"),
        P(),
        P(),
    )
    return jax.shard_map(
        on_device,
        mesh=mesh,
        in_specs=placed,
        out_specs=(P("gx", "gy", "gz"), P(("gx", "gy", "gz"))),
        check_vma=False,
    )
```
